256 devices in a mesh: dp: 8 (over x_lo, y), ctx: 32 (over x_hi, z, core).
Axes of the slice: x: 4 (x_hi: 2, x_lo: 2; x = x_hi * 2 + x_lo), y: 4, z: 8, core: 2. Of those that a mesh axis runs over, the one named last changes fastest.
Arguments:
- q_raw: bfloat16 [8, 4096, 2048], P('dp', 'ctx'), may hold values from -220 to 220
- k_raw: bfloat16 [8, 4096, 2048], P('dp', 'ctx'), may hold values from -220 to 220
- values: bfloat16 [8, 4096, 2048], P('dp', 'ctx'), may hold values from -6 to 6
- d_out: bfloat16 [8, 4096, 2048], P('dp', 'ctx'), may hold values from -14 to 14
- q_gain: float32 [2048], replicated, may hold values from 0.5 to 6
- k_gain: float32 [2048], replicated, may hold values from 0.5 to 6
Outputs:
- grad_q_raw: bfloat16 [8, 4096, 2048], P('dp', 'ctx')
- grad_k_raw: bfloat16 [8, 4096, 2048], P('dp', 'ctx')
- grad_values: bfloat16 [8, 4096, 2048], P('dp', 'ctx')
- grad_q_gain: float32 [2048], replicated
- grad_k_gain: float32 [2048], replicated
The draws below stay inside these ranges and needn't reach their ends.
All inputs are finite; a program needn't handle non-finite values.
Results may differ from the reference program's by a relative error of at most 0.013.
The reference program's roundings to bfloat16 on the way (of `queries`, `key_rows`, `weights` and `dscore`) count: a program that leaves them out, or rounds other values in their place, can miss the bound.
Values may be sent and summed in bfloat16 or wider, within the bound.
No kernel may reach another device: no remote copies, remote signals or barrier semaphores. Data moves between devices by JAX's collectives and lax.ppermute only.
A program may use at most 64 MiB of HBM per device.

```python
import math
import jax
import jax.numpy as jnp
from jax import lax

HEADS = 16
HD = 128
TILE = 64
S_DEV = 128
SEG1 = 1024
R1 = 4
R2 = 8
FEAT = 2048
SEQS = 8
LENGTH = 4096


def row_scale(key, upper):
    return jnp.exp(jax.random.uniform(key, (SEQS, LENGTH, 1), jnp.float32, 0.0, math.log(upper)))


def draw_q_raw(key, part):
    key = jax.random.fold_in(key, 3)
    own_rows = jnp.clip(jax.random.normal(jax.random.fold_in(key, 1), (SEQS, LENGTH, HEADS * HD), jnp.float32), -5.0, 5.0)
    return (own_rows * row_scale(jax.random.fold_in(key, 2), 10.0)).astype(jnp.bfloat16)


def draw_k_raw(key, part):
    key = jax.random.fold_in(key, 4)
    own_rows = jnp.clip(jax.random.normal(jax.random.fold_in(key, 1), (SEQS, LENGTH, HEADS * HD), jnp.float32), -5.0, 5.0)
    return (own_rows * row_scale(jax.random.fold_in(key, 2), 10.0)).astype(jnp.bfloat16)


def draw_q_gain(key, part):
    key = jax.random.fold_in(key, 5)
    drawn = jnp.exp(jax.random.uniform(key, (HEADS, HD), jnp.float32, math.log(0.5), math.log(2.0)))
    return drawn.reshape(HEADS * HD)


def draw_k_gain(key, part):
    key = jax.random.fold_in(key, 6)
    drawn = jnp.exp(jax.random.uniform(key, (HEADS, HD), jnp.float32, math.log(0.5), math.log(2.0)))
    return drawn.reshape(HEADS * HD)


def draw_d_out(key, part):
    key = jax.random.fold_in(key, 9)
    own_rows = jnp.clip(jax.random.normal(jax.random.fold_in(key, 1), (SEQS, LENGTH, HEADS * HD), jnp.float32), -5.0, 5.0)
    placing = (jnp.arange(SEQS)[:, None] * LENGTH + jnp.arange(LENGTH)[None, :]).astype(jnp.float32) / (SEQS * LENGTH)
    scaling = (0.3 * (1.0 + 2.0 * placing))[:, :, None]
    return (own_rows * scaling).astype(jnp.bfloat16)


def levels(own_key, shape, shards, low, top_value):
    gain = 1.0
    for position, blocks in shards:
        draws = jax.random.uniform(jax.random.fold_in(jax.random.fold_in(own_key, 6), position), (blocks,), jnp.float32, low / len(shards), top_value / len(shards))
        gain = gain * jnp.repeat(jnp.exp(draws), shape[position] // blocks).reshape((-1,) + (1,) * (len(shape) - 1 - position))
    return gain


def noise(stream_key, dims, spread, reach, split=(), kind=jnp.bfloat16):
    drawn = spread * jax.random.normal(stream_key, dims, jnp.float32)
    if split:
        drawn = drawn * levels(stream_key, dims, split, -0.22, 0.18)
    return jnp.clip(drawn, -reach, reach).astype(kind)


def setup_inputs(seed: int = 0) -> dict:
    streams_of = jax.random.split(jax.random.key(seed), 7)
    q_raw = draw_q_raw(jax.random.fold_in(streams_of[6], 71), 0)
    k_raw = draw_k_raw(jax.random.fold_in(streams_of[6], 71), 0)
    values = noise(streams_of[2], (SEQS, LENGTH, FEAT), 1.0, 6.0, ((0, 8), (1, 32)))
    d_out = draw_d_out(jax.random.fold_in(streams_of[6], 71), 0)
    q_gain = draw_q_gain(jax.random.fold_in(streams_of[6], 71), 0)
    k_gain = draw_k_gain(jax.random.fold_in(streams_of[6], 71), 0)
    return dict(q_raw=q_raw, k_raw=k_raw, values=values, d_out=d_out, q_gain=q_gain, k_gain=k_gain)


EPS = 1e-06

def product(pattern, first_arg, second_arg):
    return jnp.einsum(pattern, first_arg.astype(jnp.float32), second_arg.astype(jnp.float32), precision=lax.Precision.HIGHEST)

def normalize(raw_rows, gain_row):
    shaped = raw_rows.astype(jnp.float32).reshape(raw_rows.shape[:-1] + (HEADS, HD))
    inverse = lax.rsqrt(lax.optimization_barrier(jnp.mean(shaped * shaped, axis=-1, keepdims=True)) + EPS)
    normed = shaped * inverse
    scaled = (normed * gain_row.reshape(HEADS, HD)).astype(jnp.bfloat16)
    return (normed, inverse, scaled)

def norm_grad(upstream, normed, inverse, gain_row):
    weighted = upstream * gain_row.reshape(HEADS, HD)
    inner_dot = lax.optimization_barrier(jnp.mean(weighted * normed, axis=-1, keepdims=True))
    result = inverse * (weighted - normed * inner_dot)
    return result.reshape(result.shape[:-2] + (HEADS * HD,)).astype(jnp.bfloat16)

def to_compact(full, dilation):
    trailing = full.shape[2:]
    groups = LENGTH // (TILE * dilation)
    shared = HEADS // dilation
    shaped = full.reshape((groups, dilation, TILE, shared, dilation) + trailing)
    diagonal = jnp.diagonal(shaped, axis1=1, axis2=4)
    diagonal = jnp.moveaxis(diagonal, -1, 0)
    diagonal = jnp.moveaxis(diagonal, 3, 1)
    return diagonal.reshape((dilation, shared, groups * TILE) + trailing)

def from_compact(compact, dilation, fill_value):
    trailing = compact.shape[3:]
    groups = LENGTH // (TILE * dilation)
    shared = HEADS // dilation
    shaped = compact.reshape((dilation, shared, groups, TILE) + trailing)
    shaped = jnp.moveaxis(shaped, 1, 3)
    shaped = jnp.moveaxis(shaped, 0, 1)
    expanded = shaped[:, :, :, :, None]
    matching = jnp.arange(dilation)[:, None] == jnp.arange(dilation)[None, :]
    eye_mask = matching.reshape((1, dilation, 1, 1, dilation) + (1,) * len(trailing))
    placed = jnp.where(eye_mask, expanded, jnp.asarray(fill_value, compact.dtype))
    return placed.reshape((LENGTH, HEADS) + trailing)

def to_level(full, dilation, seg_rows):
    compact = to_compact(full, dilation)
    return compact.reshape(compact.shape[:2] + (compact.shape[2] // seg_rows, seg_rows) + compact.shape[3:])

def to_full(level_array, dilation, fill_value):
    flattened = level_array.reshape(level_array.shape[:2] + (-1,) + level_array.shape[4:])
    return from_compact(flattened, dilation, fill_value)

def pair_sum(weights, rows, dilation, seg_rows, factor):
    if dilation == 1:
        return factor * product('abnij,abnid->abnjd', weights, rows)
    lead = weights.shape[:3]
    tile_count = seg_rows // TILE
    split_weights = weights.reshape(lead + (tile_count, TILE, tile_count, TILE))
    split_rows = rows.reshape(lead + (tile_count, TILE, HD))
    pair_terms = factor * product('abnpiqj,abnpid->abnpqjd', split_weights, split_rows)
    own_pair = (jnp.arange(tile_count)[:, None] == jnp.arange(tile_count)[None, :]).reshape(1, 1, 1, tile_count, tile_count, 1, 1)
    rounded = lax.optimization_barrier(pair_terms.astype(jnp.bfloat16)).astype(jnp.float32)
    chosen = jnp.where(own_pair, pair_terms, rounded)
    return lax.optimization_barrier(jnp.sum(chosen, axis=3)).reshape(lead + (seg_rows, HD))

def sequence_grads(q_raw, k_raw, values, d_out, q_gain, k_gain):
    normed_q, inverse_q, queries = normalize(q_raw, q_gain)
    normed_k, inverse_k, key_rows = normalize(k_raw, k_gain)
    value_rows = values.reshape(LENGTH, HEADS, HD)
    grad_out = d_out.reshape(LENGTH, HEADS, HD)
    score_scale = HD ** (-0.5)
    level_data = []
    for dilation, segment in ((1, S_DEV), (R1, SEG1), (R2, LENGTH)):
        seg_rows = segment // dilation
        level_q = to_level(queries, dilation, seg_rows)
        level_k = to_level(key_rows, dilation, seg_rows)
        level_v = to_level(value_rows, dilation, seg_rows)
        level_g = to_level(grad_out, dilation, seg_rows)
        causal = jnp.tril(jnp.ones((seg_rows, seg_rows), dtype=bool))
        scores = jnp.where(causal, product('abnid,abnjd->abnij', level_q, level_k) * score_scale, -jnp.inf)
        level_data.append((dilation, seg_rows, level_q, level_k, level_v, level_g, scores))
    row_max = jnp.full((LENGTH, HEADS), -jnp.inf, jnp.float32)
    for dilation, seg_rows, level_q, level_k, level_v, level_g, scores in level_data:
        row_max = jnp.maximum(row_max, to_full(lax.optimization_barrier(jnp.max(scores, axis=-1)), dilation, -jnp.inf))
    row_total = jnp.zeros((LENGTH, HEADS), jnp.float32)
    for dilation, seg_rows, level_q, level_k, level_v, level_g, scores in level_data:
        shift_by = to_level(row_max, dilation, seg_rows)
        row_total = row_total + to_full(lax.optimization_barrier(jnp.sum(jnp.exp(scores - shift_by[..., None]), axis=-1)), dilation, 0.0)
    log_total = row_max + jnp.log(row_total)
    attn_out = jnp.zeros((LENGTH, HEADS, HD), jnp.float32)
    level_probs = []
    for dilation, seg_rows, level_q, level_k, level_v, level_g, scores in level_data:
        level_prob = jnp.exp(scores - to_level(log_total, dilation, seg_rows)[..., None])
        level_weight = level_prob.astype(jnp.bfloat16)
        attn_out = attn_out + to_full(product('abnij,abnjd->abnid', level_weight, level_v), dilation, 0.0)
        level_probs.append((level_prob, level_weight))
    row_dot = lax.optimization_barrier(jnp.sum(grad_out.astype(jnp.float32) * attn_out, axis=2))
    query_sum = jnp.zeros((LENGTH, HEADS, HD), jnp.float32)
    key_grad = jnp.zeros((LENGTH, HEADS, HD), jnp.float32)
    value_grad = jnp.zeros((LENGTH, HEADS, HD), jnp.float32)
    for level_tuple, prob_pair in zip(level_data, level_probs):
        dilation, seg_rows, level_q, level_k, level_v, level_g, scores = level_tuple
        level_prob, level_weight = prob_pair
        level_dot = to_level(row_dot, dilation, seg_rows)
        dscore = (level_prob * (product('abnid,abnjd->abnij', level_g, level_v) - level_dot[..., None])).astype(jnp.bfloat16)
        query_sum = query_sum + to_full(product('abnij,abnjd->abnid', dscore, level_k), dilation, 0.0)
        key_grad = key_grad + to_full(pair_sum(dscore, level_q, dilation, seg_rows, score_scale), dilation, 0.0)
        value_grad = value_grad + to_full(pair_sum(level_weight, level_g, dilation, seg_rows, 1.0), dilation, 0.0)
    query_grad = score_scale * query_sum
    query_terms = lax.optimization_barrier(jnp.sum(query_grad * normed_q, axis=0))
    key_terms = lax.optimization_barrier(jnp.sum(key_grad * normed_k, axis=0))
    return (norm_grad(query_grad, normed_q, inverse_q, q_gain), norm_grad(key_grad, normed_k, inverse_k, k_gain), value_grad.astype(jnp.bfloat16).reshape(LENGTH, HEADS * HD), query_terms, key_terms)

def reference(q_raw, k_raw, values, d_out, q_gain, k_gain):
    outputs = lax.map(lambda pieces: sequence_grads(pieces[0], pieces[1], pieces[2], pieces[3], q_gain, k_gain), (q_raw, k_raw, values, d_out))
    grad_q, grad_k, grad_v, query_terms, key_terms = outputs
    return (grad_q, grad_k, grad_v, lax.optimization_barrier(jnp.sum(query_terms, axis=0)).reshape(HEADS * HD), lax.optimization_barrier(jnp.sum(key_terms, axis=0)).reshape(HEADS * HD))
```

```python
import jax
import jax.numpy as jnp
from jax import lax
from jax.experimental import pallas as pl
from jax.experimental.pallas import tpu as pltpu
from jax.sharding import PartitionSpec as P

HEADS = 16
HD = 128
TILE = 64
ROWS = 128
EPS = 1e-06
SCALE = HD ** (-0.5)
BF = jnp.bfloat16
F32 = jnp.float32
NEG = -jnp.inf


def vmem_spec():
    return pl.BlockSpec(memory_space=pltpu.VMEM)


def smem_spec():
    return pl.BlockSpec(memory_space=pltpu.SMEM)


def any_spec():
    return pl.BlockSpec(memory_space=pl.ANY)


def place(c):
    core = c & 1
    zl = (c >> 1) & 3
    zh = (c >> 3) & 1
    xh = (c >> 4) & 1
    return core, zl, zh, xh


def owned_heads(c, k):
    core, zl, zh, xh = place(c)
    rank = (zl ^ (2 * zh)) ^ k
    par = rank & 1
    base = 2 * core + 8 * (rank >> 1)
    return base + 4 * par, base + 1 + 4 * (1 - par)


def normalize(raw, gain):
    x = raw.astype(F32)
    inverse = lax.rsqrt(jnp.mean(x * x, axis=-1, keepdims=True) + EPS)
    normed = x * inverse
    return normed, inverse, (normed * gain).astype(BF)


def norm_grad(upstream, normed, inverse, gain):
    weighted = upstream * gain
    inner = jnp.mean(weighted * normed, axis=-1, keepdims=True)
    return (inverse * (weighted - normed * inner)).astype(BF)


def dot_nt(a, b):
    return lax.dot_general(a, b, (((1,), (1,)), ((), ())), preferred_element_type=F32)


def dot_nn(a, b):
    return lax.dot_general(a, b, (((1,), (0,)), ((), ())), preferred_element_type=F32)


def dot_tn(a, b):
    return lax.dot_general(a, b, (((0,), (0,)), ((), ())), preferred_element_type=F32)


def pack_kernel(c_ref, q, k, v, g, m0, m1, m2, m3, sems):
    c = c_ref[0]
    copies = []
    for step, out in enumerate((m0, m1, m2, m3)):
        h0, h1 = owned_heads(c, step)
        tiles = (
            (q, 0, h0), (g, 0, h0), (k, 0, h0), (v, 0, h0),
            (q, 1, h1), (g, 1, h1), (k, 1, h1), (v, 1, h1),
            (k, 0, h1), (v, 0, h1),
        )
        for t, (src, e, h) in enumerate(tiles):
            copy = pltpu.make_async_copy(
                src.at[pl.ds(e * TILE, TILE), pl.ds(pl.multiple_of(h * HD, HD), HD)],
                out.at[pl.ds(t * TILE, TILE), :],
                sems.at[step, t],
            )
            copy.start()
            copies.append(copy)
    for copy in copies:
        copy.wait()


def forward_pack_kernel(r0, r1, r2, r3, out, sems):
    copies = []
    for k, (src, at) in enumerate(((r0, 2), (r2, 2), (r1, 6), (r3, 6))):
        copy = pltpu.make_async_copy(
            src.at[pl.ds(at * TILE, 2 * TILE), :], out.at[pl.ds(2 * k * TILE, 2 * TILE), :], sems.at[k]
        )
        copy.start()
        copies.append(copy)
    for copy in copies:
        copy.wait()


def home_kernel(
    c_ref, q, k, v, g, q_gain, k_gain, gq_out, gk_out, gv_out, part_k, part_v, gains, dk_all, dv_all
):
    c = c_ref[0]
    core = c & 1
    row = lax.broadcasted_iota(jnp.int32, (ROWS, ROWS), 0)
    col = lax.broadcasted_iota(jnp.int32, (ROWS, ROWS), 1)
    causal = col <= row
    tile_of_row = lax.broadcasted_iota(jnp.int32, (ROWS, 1), 0) // TILE
    for h in range(HEADS):
        cols = slice(h * HD, (h + 1) * HD)
        kind = h % 4
        owned = (tile_of_row == (kind & 1)) & (core == (kind >> 1))
        keep = jnp.where(owned, 0.0, 1.0)
        qg = q_gain[h : h + 1, :]
        kg = k_gain[h : h + 1, :]
        qn, q_inv, qb = normalize(q[:, cols], qg)
        kn, k_inv, kb = normalize(k[:, cols], kg)
        vb = v[:, cols]
        gb = g[:, cols]
        s = jnp.where(causal, dot_nt(qb, kb) * SCALE, NEG)
        top = jnp.max(s, axis=1, keepdims=True)
        total = jnp.sum(jnp.exp(s - top), axis=1, keepdims=True)
        p = jnp.exp(s - (top + jnp.log(total))) * keep
        w = p.astype(BF)
        dp = dot_nt(gb, vb)
        row_dot = jnp.sum(w.astype(F32) * dp, axis=1, keepdims=True)
        ds = (p * (dp - row_dot)).astype(BF)
        dq = dot_nn(ds, kb) * SCALE
        dk = dot_tn(ds, qb) * SCALE
        dv = dot_tn(w, gb)
        gq_out[:, cols] = norm_grad(dq, qn, q_inv, qg)
        gk_out[:, cols] = norm_grad(dk, kn, k_inv, kg)
        gv_out[:, cols] = dv.astype(BF)
        dk_all[h] = dk
        dv_all[h] = dv
        gains[h : h + 1, :] = jnp.sum(dq * qn, axis=0, keepdims=True)
        gains[HEADS + h : HEADS + h + 1, :] = jnp.sum(dk * kn, axis=0, keepdims=True)
    for step in range(4):
        h0, h1 = owned_heads(c, step)
        for i, (h, e) in enumerate(((h0, 0), (h1, 1), (h1, 0))):
            rows = slice(e * TILE, (e + 1) * TILE)
            part_k[3 * step + i] = dk_all[h, rows, :]
            part_v[3 * step + i] = dv_all[h, rows, :]


def owner_kernel(
    c_ref, r0, r1, r2, r3, b1, b2, b3, q_gain, k_gain, home_gains,
    x0, x1, x2, x3, t1, t2, t3, far_k, far_v, gains,
):
    c = c_ref[0]
    core, zl, zh, xh = place(c)
    heads = owned_heads(c, 0)
    received = (r0, r1, r2, r3)
    crossed = (b1, b2, b3)
    returned = (x0, x1, x2, x3)
    terms = (t1, t2, t3)
    live = (zh == 1, xh == 1, xh == 1)
    gains[...] = home_gains[...]
    row = lax.broadcasted_iota(jnp.int32, (TILE, TILE), 0)
    col = lax.broadcasted_iota(jnp.int32, (TILE, TILE), 1)
    lower = col <= row

    def rows_of(ref, tile, count=1):
        return ref[tile * TILE : (tile + count) * TILE, :]

    for e in range(2):
        base = 4 * e
        far = (e, e + 2)
        h = heads[e]
        qg = q_gain[pl.ds(h, 1), :]
        kg = k_gain[pl.ds(h, 1), :]
        q_raw = jnp.concatenate([rows_of(r, base) for r in received], axis=0)
        gb = jnp.concatenate([rows_of(r, base + 1) for r in received], axis=0)
        k_parts = [rows_of(r, base + 2) for r in received]
        v_parts = [rows_of(r, base + 3) for r in received]
        for b in crossed:
            k_parts += [rows_of(b, base), rows_of(b, base + 2)]
            v_parts += [rows_of(b, base + 1), rows_of(b, base + 3)]
        if e == 1:
            k_parts += [rows_of(r, 8) for r in received]
            v_parts += [rows_of(r, 9) for r in received]
        k_raw = jnp.concatenate(k_parts, axis=0)
        vb = jnp.concatenate(v_parts, axis=0)
        qn, q_inv, qb = normalize(q_raw, qg)
        kn, k_inv, kb = normalize(k_raw, kg)
        p_rows = []
        w_blocks = []
        ds_blocks = []
        for i in range(4):
            rows = slice(i * TILE, (i + 1) * TILE)
            is_far = i in far
            spans = [(0, 256)]
            if is_far:
                spans.append((256, 640))
            if e == 1:
                spans.append((640 + i * TILE, 640 + (i + 1) * TILE))
            counts = []
            for j in range(4):
                if i == j:
                    counts.append(jnp.where(lower, 3.0 if is_far else 2.0, 0.0))
                else:
                    both = 2.0 if is_far and j in far else 1.0
                    earlier = (zl ^ j) < (zl ^ i)
                    counts.append(jnp.full((TILE, TILE), jnp.where(earlier, both, 0.0), F32))
            if is_far:
                for m in range(3):
                    counts.append(jnp.full((TILE, 2 * TILE), jnp.where(live[m], 1.0, 0.0), F32))
            if e == 1:
                counts.append(jnp.ones((TILE, TILE), F32))
            count = jnp.concatenate(counts, axis=1)
            keys = jnp.concatenate([kb[a:b] for a, b in spans], axis=0)
            vals = jnp.concatenate([vb[a:b] for a, b in spans], axis=0)
            s = jnp.where(count > 0.0, dot_nt(qb[rows], keys) * SCALE, NEG)
            dp = dot_nt(gb[rows], vals)
            top = jnp.max(s, axis=1, keepdims=True)
            total = jnp.sum(count * jnp.exp(s - top), axis=1, keepdims=True)
            p = count * jnp.exp(s - (top + jnp.log(total)))
            w = p.astype(BF)
            row_dot = jnp.sum(w.astype(F32) * dp, axis=1, keepdims=True)
            ds = (p * (dp - row_dot)).astype(BF)
            p_rows.append(dot_nn(ds, keys))
            w_blocks.append(w)
            ds_blocks.append(ds)
        dq = jnp.concatenate(p_rows, axis=0) * SCALE
        ds_own = jnp.concatenate([d[:, :256] for d in ds_blocks], axis=0)
        w_own = jnp.concatenate([w[:, :256] for w in w_blocks], axis=0)
        dk_own = dot_tn(ds_own, qb) * SCALE
        dv_own = dot_tn(w_own, gb)
        ds_far = jnp.concatenate([ds_blocks[i][:, 256:640] for i in far], axis=0)
        w_far = jnp.concatenate([w_blocks[i][:, 256:640] for i in far], axis=0)
        q_far = jnp.concatenate([qb[i * TILE : (i + 1) * TILE] for i in far], axis=0)
        g_far = jnp.concatenate([gb[i * TILE : (i + 1) * TILE] for i in far], axis=0)
        dk_far = dot_tn(ds_far, q_far) * SCALE
        dv_far = dot_tn(w_far, g_far)
        key_sum = jnp.sum(dk_own * kn[:256], axis=0, keepdims=True)
        key_sum += jnp.sum(dk_far * kn[256:640], axis=0, keepdims=True)
        gq = norm_grad(dq, qn, q_inv, qg)
        for i in range(4):
            rows = slice(i * TILE, (i + 1) * TILE)
            out = returned[i]
            out[3 * e * TILE : (3 * e + 1) * TILE, :] = gq[rows]
            out[(3 * e + 1) * TILE : (3 * e + 2) * TILE, :] = dk_own[rows].astype(BF)
            out[(3 * e + 2) * TILE : (3 * e + 3) * TILE, :] = dv_own[rows].astype(BF)
            if i in far:
                far_k[i] = dk_own[rows]
                far_v[i] = dv_own[rows]
            if e == 1:
                ds_x = ds_blocks[i][:, -TILE:]
                dk_x = dot_tn(ds_x, qb[rows]) * SCALE
                dv_x = dot_tn(w_blocks[i][:, -TILE:], gb[rows])
                key_sum += jnp.sum(dk_x * kn[640 + i * TILE : 704 + i * TILE], axis=0, keepdims=True)
                out[6 * TILE : 7 * TILE, :] = dk_x.astype(BF)
                out[7 * TILE : 8 * TILE, :] = dv_x.astype(BF)
        for m in range(3):
            rows = slice(m * 128, (m + 1) * 128)
            terms[m][256 * e : 256 * e + 128, :] = dk_far[rows].astype(BF)
            terms[m][256 * e + 128 : 256 * e + 256, :] = dv_far[rows].astype(BF)
        gains[pl.ds(h, 1), :] += jnp.sum(dq * qn, axis=0, keepdims=True)
        gains[pl.ds(HEADS + h, 1), :] += key_sum


def return_pack_kernel(far_k, far_v, u1, u2, u3, x0, x1, x2, x3, y0, y1, y2, y3):
    for i, (x, y) in enumerate(((x0, y0), (x1, y1), (x2, y2), (x3, y3))):
        e = i & 1
        at = 256 * e + 64 * (i >> 1)
        dk = far_k[i]
        dv = far_v[i]
        for u in (u1, u2, u3):
            dk += u[at : at + TILE, :].astype(F32)
            dv += u[at + 128 : at + 128 + TILE, :].astype(F32)
        first = (3 * e + 1) * TILE
        y[0:first, :] = x[0:first, :]
        y[first : first + TILE, :] = dk.astype(BF)
        y[first + TILE : first + 2 * TILE, :] = dv.astype(BF)
        y[first + 2 * TILE :, :] = x[first + 2 * TILE :, :]


def final_kernel(
    c_ref, y0, y1, y2, y3, m0, m1, m2, m3, part_k, part_v, k_gain, gq_in, gk_in, gv_in,
    gq_out, gk_out, gv_out, raw, done_k, done_v, sems, raw_sems,
):
    c = c_ref[0]
    copies = []

    def send(src, dst, e, h, n):
        copy = pltpu.make_async_copy(
            src, dst.at[pl.ds(e * TILE, TILE), pl.ds(pl.multiple_of(h * HD, HD), HD)], sems.at[n]
        )
        copy.start()
        copies.append(copy)

    sent = (m0, m1, m2, m3)
    fetches = []
    for step in range(4):
        for i, tile in enumerate((2, 6, 8)):
            copy = pltpu.make_async_copy(
                sent[step].at[pl.ds(tile * TILE, TILE), :], raw.at[3 * step + i], raw_sems.at[3 * step + i]
            )
            copy.start()
            fetches.append(copy)
    for step, y in enumerate((y0, y1, y2, y3)):
        h0, h1 = owned_heads(c, step)
        send(y.at[pl.ds(0, TILE), :], gq_out, 0, h0, 8 * step)
        send(y.at[pl.ds(3 * TILE, TILE), :], gq_out, 1, h1, 8 * step + 1)
        for i, (h, e, at) in enumerate(((h0, 0, 1), (h1, 1, 4), (h1, 0, 6))):
            n = 3 * step + i
            fetches[n].wait()
            kg = k_gain[pl.ds(h, 1), :]
            kn, k_inv, _ = normalize(raw[n], kg)
            dk = part_k[n] + y[at * TILE : (at + 1) * TILE, :].astype(F32)
            dv = part_v[n] + y[(at + 1) * TILE : (at + 2) * TILE, :].astype(F32)
            done_k[n] = norm_grad(dk, kn, k_inv, kg)
            done_v[n] = dv.astype(BF)
            send(done_k.at[n], gk_out, e, h, 8 * step + 2 + 2 * i)
            send(done_v.at[n], gv_out, e, h, 8 * step + 3 + 2 * i)
    for copy in copies:
        copy.wait()


def per_device(q_raw, k_raw, values, d_out, q_gain, k_gain):
    ctx_count = lax.axis_size("ctx")
    dp_count = lax.axis_size("dp")
    here = lax.axis_index("ctx").astype(jnp.int32).reshape(1)
    flat = lambda a: a.reshape(ROWS, HEADS * HD)
    q, k, v, g = flat(q_raw), flat(k_raw), flat(values), flat(d_out)
    qg = q_gain.reshape(HEADS, HD)
    kg = k_gain.reshape(HEADS, HD)
    params = pltpu.CompilerParams(vmem_limit_bytes=48 * 1024 * 1024)
    shape = jax.ShapeDtypeStruct

    def swap(block, axis, mask):
        count = ctx_count if axis == "ctx" else dp_count
        return lax.ppermute(block, axis, [(i, i ^ mask) for i in range(count)])

    def sends_on(a, b):
        return ((a >> 3) & 3) < ((b >> 3) & 3)

    steps = (12, 16, 28)

    def forward(block, mask):
        route = [(i, i ^ mask) for i in range(ctx_count) if sends_on(i, i ^ mask)]
        return lax.ppermute(block, "ctx", route)

    def backward(block, mask):
        route = [(i, i ^ mask) for i in range(ctx_count) if sends_on(i ^ mask, i)]
        return lax.ppermute(block, "ctx", route)

    packed = pl.pallas_call(
        pack_kernel,
        in_specs=[smem_spec()] + [any_spec()] * 4,
        out_specs=[any_spec()] * 4,
        out_shape=[shape((10 * TILE, HD), BF)] * 4,
        scratch_shapes=[pltpu.SemaphoreType.DMA((4, 10))],
        compiler_params=params,
        name="pack_tiles",
    )(here, q, k, v, g)
    arrived = [packed[0]] + [swap(packed[i], "ctx", 2 * i) for i in (1, 2, 3)]

    gq_home, gk_home, gv_home, part_k, part_v, home_gains = pl.pallas_call(
        home_kernel,
        in_specs=[smem_spec()] + [vmem_spec()] * 6,
        out_specs=[vmem_spec()] * 6,
        out_shape=[shape((ROWS, HEADS * HD), BF)] * 3
        + [shape((12, TILE, HD), F32)] * 2
        + [shape((2 * HEADS, HD), F32)],
        scratch_shapes=[pltpu.VMEM((HEADS, ROWS, HD), F32)] * 2,
        compiler_params=params,
        name="home_slab",
    )(here, q, k, v, g, qg, kg)

    onward = pl.pallas_call(
        forward_pack_kernel,
        in_specs=[any_spec()] * 4,
        out_specs=any_spec(),
        out_shape=shape((8 * TILE, HD), BF),
        scratch_shapes=[pltpu.SemaphoreType.DMA((4,))],
        compiler_params=params,
        name="pack_far_rows",
    )(*arrived)
    crossed = [forward(onward, mask) for mask in steps]

    outs = pl.pallas_call(
        owner_kernel,
        in_specs=[smem_spec()] + [vmem_spec()] * 10,
        out_specs=[vmem_spec()] * 10,
        out_shape=[shape((8 * TILE, HD), BF)] * 7
        + [shape((4, TILE, HD), F32)] * 2
        + [shape((2 * HEADS, HD), F32)],
        compiler_params=params,
        name="owned_heads",
    )(here, *arrived, *crossed, qg, kg, home_gains)
    back, terms, far_k, far_v, gains = outs[:4], outs[4:7], outs[7], outs[8], outs[9]
    terms_in = [backward(terms[i], mask) for i, mask in enumerate(steps)]

    def pair_sum(x, axis, mask):
        return x + swap(x, axis, mask)

    def quad_sum(x, axis, mask):
        one, two, three = (swap(x, axis, i * mask) for i in (1, 2, 3))
        return (x + one) + (two + three)

    gains = pair_sum(gains, "ctx", 1)
    if dp_count == 8:
        gains = quad_sum(gains, "dp", 1)
        gains = pair_sum(gains, "dp", 4)
    gains = quad_sum(gains, "ctx", 2)
    gains = pair_sum(gains, "ctx", 12)
    gains = pair_sum(gains, "ctx", 16)

    back = pl.pallas_call(
        return_pack_kernel,
        in_specs=[vmem_spec()] * 9,
        out_specs=[vmem_spec()] * 4,
        out_shape=[shape((8 * TILE, HD), BF)] * 4,
        compiler_params=params,
        name="add_far_terms",
    )(far_k, far_v, *terms_in, *back)
    home = [back[0]] + [swap(back[i], "ctx", 2 * i) for i in (1, 2, 3)]

    gq, gk, gv = pl.pallas_call(
        final_kernel,
        in_specs=[smem_spec()]
        + [vmem_spec()] * 4
        + [any_spec()] * 4
        + [vmem_spec()] * 3
        + [any_spec()] * 3,
        out_specs=[any_spec()] * 3,
        out_shape=[shape((ROWS, HEADS * HD), BF)] * 3,
        scratch_shapes=[pltpu.VMEM((12, TILE, HD), BF)] * 3
        + [pltpu.SemaphoreType.DMA((32,)), pltpu.SemaphoreType.DMA((12,))],
        input_output_aliases={12: 0, 13: 1, 14: 2},
        compiler_params=params,
        name="finish_rows",
    )(here, *home, *packed, part_k, part_v, kg, gq_home, gk_home, gv_home)
    whole = lambda a: a.reshape(1, ROWS, HEADS * HD)
    return (
        whole(gq),
        whole(gk),
        whole(gv),
        gains[:HEADS].reshape(HEADS * HD),
        gains[HEADS:].reshape(HEADS * HD),
    )


def solution(mesh):
    rows = P("dp", "ctx", None)
    return jax.shard_map(
        per_device,
        mesh=mesh,
        in_specs=(rows, rows, rows, rows, P(), P()),
        out_specs=(rows, rows, rows, P(), P()),
        check_vma=False,
    )
```

```python
import functools

import jax
import jax.numpy as jnp
from jax import lax
from jax.experimental import pallas as pl
from jax.experimental.pallas import tpu as pltpu
from jax.sharding import PartitionSpec as P

HEADS = 16
HD = 128
TILE = 64
ROWS = 128
EPS = 1e-06
SCALE = HD ** (-0.5)
BF = jnp.bfloat16
F32 = jnp.float32
NEG = -jnp.inf
LOG_SCALE = SCALE * 1.4426950408889634


def vmem_spec():
    return pl.BlockSpec(memory_space=pltpu.VMEM)


def smem_spec():
    return pl.BlockSpec(memory_space=pltpu.SMEM)


def hbm_spec():
    return pl.BlockSpec(memory_space=pltpu.HBM)


def any_spec():
    return pl.BlockSpec(memory_space=pl.ANY)


def place(c):
    core = c & 1
    zl = (c >> 1) & 3
    zh = (c >> 3) & 1
    xh = (c >> 4) & 1
    return core, zl, zh, xh


def owned_heads(c, k):
    core, zl, zh, xh = place(c)
    rank = (zl ^ (2 * zh)) ^ k
    par = rank & 1
    base = 2 * core + 8 * (rank >> 1)
    return base + 4 * par, base + 1 + 4 * (1 - par)


def normalize(raw, gain):
    x = raw.astype(F32)
    inverse = lax.rsqrt(jnp.mean(x * x, axis=-1, keepdims=True) + EPS)
    normed = x * inverse
    return normed, inverse, (normed * gain).astype(BF)


def norm_grad(upstream, normed, inverse, gain):
    weighted = upstream * gain
    inner = jnp.mean(weighted * normed, axis=-1, keepdims=True)
    return (inverse * (weighted - normed * inner)).astype(BF)


def dot_nt(a, b):
    return lax.dot_general(a, b, (((1,), (1,)), ((), ())), preferred_element_type=F32)


def dot_nn(a, b):
    return lax.dot_general(a, b, (((1,), (0,)), ((), ())), preferred_element_type=F32)


def dot_tn(a, b):
    return lax.dot_general(a, b, (((0,), (0,)), ((), ())), preferred_element_type=F32)


def pack_kernel(early, c_ref, q, k, v, g, *refs):
    outs, sems = refs[-5:-1], refs[-1]
    c = c_ref[0]
    copies = []
    for step, out in enumerate(outs):
        heads = owned_heads(c, step)
        far = step & 1
        near = 1 - far
        if early:
            tiles = ((k, far), (v, far))
        else:
            tiles = ((q, far), (g, far), (q, near), (g, near), (k, near), (v, near), (k, 2), (v, 2))
        for t, (src, e) in enumerate(tiles):
            row = 0 if e == 2 else e * TILE
            h = heads[min(e, 1)]
            copy = pltpu.make_async_copy(
                src.at[pl.ds(row, TILE), pl.ds(pl.multiple_of(h * HD, HD), HD)],
                out.at[pl.ds(t * TILE, TILE), :],
                sems.at[len(copies)],
            )
            copy.start()
            copies.append(copy)
    for copy in copies:
        copy.wait()


def split_gains(total):
    high = total.astype(BF)
    return high, (total - high.astype(F32)).astype(BF)


def joined_gains(ref):
    at = ref.shape[0] - 64
    return ref[at : at + 32, :].astype(F32) + ref[at + 32 : at + 64, :].astype(F32)


def forward_pack_kernel(f0, f2, f3, f1, out, sems):
    copies = []
    for k, src in enumerate((f0, f2, f1, f3)):
        copy = pltpu.make_async_copy(src, out.at[pl.ds(2 * k * TILE, 2 * TILE), :], sems.at[k])
        copy.start()
        copies.append(copy)
    for copy in copies:
        copy.wait()


def home_kernel(half, c_ref, q, k, v, g, q_gain, k_gain, *refs):
    refs = refs[3 * half :]
    outs, part_k, part_v, gains = refs[:3], refs[3], refs[4], refs[5]
    loads, stores, dk_all, dv_all, in_sems, out_sems = refs[6:]
    c = c_ref[0]
    core = c & 1
    count = HEADS // 2
    group = 4
    first = half * count
    for n in range(count // group):
        cols = pl.ds((first + n * group) * HD, group * HD)
        for i, src in enumerate((q, k, v, g)):
            pltpu.make_async_copy(
                src.at[:, cols], loads.at[i, :, pl.ds(n * group * HD, group * HD)], in_sems.at[n, i]
            ).start()
    row = lax.broadcasted_iota(jnp.int32, (ROWS, ROWS), 0)
    col = lax.broadcasted_iota(jnp.int32, (ROWS, ROWS), 1)
    causal = col <= row
    tile_of_row = lax.broadcasted_iota(jnp.int32, (ROWS, 1), 0) // TILE
    copies = []
    for n in range(count // group):
        cols = pl.ds((first + n * group) * HD, group * HD)
        here = pl.ds(n * group * HD, group * HD)
        for i, src in enumerate((q, k, v, g)):
            pltpu.make_async_copy(src.at[:, cols], loads.at[i, :, here], in_sems.at[n, i]).wait()
        locs = [n * group + i for i in range(group)]
        spans = [slice(l * HD, (l + 1) * HD) for l in locs]
        qg = [q_gain[first + l : first + l + 1, :] for l in locs]
        kg = [k_gain[first + l : first + l + 1, :] for l in locs]
        qs = [normalize(loads[0, :, sp], x) for sp, x in zip(spans, qg)]
        ks = [normalize(loads[1, :, sp], x) for sp, x in zip(spans, kg)]
        vb = [loads[2, :, sp] for sp in spans]
        gb = [loads[3, :, sp] for sp in spans]
        s = [jnp.where(causal, dot_nt(x[2], y[2]), NEG) for x, y in zip(qs, ks)]
        dp = [dot_nt(x, y) for x, y in zip(gb, vb)]
        top = [jnp.max(x, axis=1, keepdims=True) for x in s]
        p = [jnp.exp2((x - t) * LOG_SCALE) for x, t in zip(s, top)]
        total = [jnp.sum(x, axis=1, keepdims=True) for x in p]
        keep = []
        for l in locs:
            kind = (first + l) % 4
            owned = (tile_of_row == (kind & 1)) & (core == (kind >> 1))
            keep.append(jnp.where(owned, 0.0, 1.0))
        p = [x * (z / t) for x, z, t in zip(p, keep, total)]
        w = [x.astype(BF) for x in p]
        rd = [jnp.sum(x.astype(F32) * y, axis=1, keepdims=True) for x, y in zip(w, dp)]
        ds = [(x * (y - z)).astype(BF) for x, y, z in zip(p, dp, rd)]
        dq = [dot_nn(x, y[2]) * SCALE for x, y in zip(ds, ks)]
        dk = [dot_tn(x, y[2]) * SCALE for x, y in zip(ds, qs)]
        dv = [dot_tn(x, y) for x, y in zip(w, gb)]
        for i, (l, sp) in enumerate(zip(locs, spans)):
            stores[0, :, sp] = norm_grad(dq[i], qs[i][0], qs[i][1], qg[i])
            stores[1, :, sp] = norm_grad(dk[i], ks[i][0], ks[i][1], kg[i])
            stores[2, :, sp] = dv[i].astype(BF)
            dk_all[l] = dk[i]
            dv_all[l] = dv[i]
            gains[l : l + 1, :] = jnp.sum(dq[i] * qs[i][0], axis=0, keepdims=True)
            gains[count + l : count + l + 1, :] = jnp.sum(dk[i] * ks[i][0], axis=0, keepdims=True)
        for i, dst in enumerate(outs):
            copy = pltpu.make_async_copy(stores.at[i, :, here], dst.at[:, cols], out_sems.at[n, i])
            copy.start()
            copies.append(copy)
    for j in range(2):
        h0 = 2 * core + 4 * j
        h1 = 2 * core + 1 + 4 * (1 - j)
        for i, (h, e) in enumerate(((h0, 0), (h1, 1), (h1, 0))):
            rows = slice(e * TILE, (e + 1) * TILE)
            part_k[3 * j + i] = dk_all[h, rows, :]
            part_v[3 * j + i] = dv_all[h, rows, :]
    for copy in copies:
        copy.wait()


def owner_kernel(
    c_ref, f0, f2, f3, f1, r0, r2, r3, r1, b1, b2, b3, q_gain, k_gain, low_gains, high_gains,
    x0, x1, x2, x3, t1, t2, t3, far_k, far_v, gains_out, gains,
):
    c = c_ref[0]
    core, zl, zh, xh = place(c)
    heads = owned_heads(c, 0)
    early = (f0, f1, f2, f3)
    late = (r0, r1, r2, r3)
    crossed = (b1, b2, b3)
    returned = (x0, x1, x2, x3)
    terms = (t1, t2, t3)
    live = (xh == 1, zh == 1, xh == 1)
    half = HEADS // 2
    for at, src in ((0, low_gains), (half, high_gains)):
        gains[at : at + half, :] = src[0:half, :]
        gains[HEADS + at : HEADS + at + half, :] = src[half:, :]
    row = lax.broadcasted_iota(jnp.int32, (TILE, 4 * TILE), 0)
    col = lax.broadcasted_iota(jnp.int32, (TILE, 4 * TILE), 1)
    block = col >> 6
    lower = (col & (TILE - 1)) <= row
    far_block = lax.broadcasted_iota(jnp.int32, (1, 6 * TILE), 1) >> 7
    bias = [jnp.where(x, 0.0, NEG) for x in live]
    far_bias = jnp.where(far_block == 0, bias[0], jnp.where(far_block == 1, bias[1], bias[2]))

    def rows_of(ref, tile):
        return ref[tile * TILE : (tile + 1) * TILE, :]

    both = (0, 1)
    order = ((0, 2, 1, 3), (1, 3, 0, 2))
    qg = [q_gain[pl.ds(h, 1), :] for h in heads]
    kg = [k_gain[pl.ds(h, 1), :] for h in heads]


    def stack(e, t):
        parts = []
        for a, i in enumerate(order[e]):
            if a < 2:
                parts.append(rows_of(late[i], t) if t < 2 else rows_of(early[i], t - 2))
            else:
                parts.append(rows_of(late[i], 2 + t))
        return jnp.concatenate(parts, axis=0)

    qs = [normalize(stack(e, 0), qg[e]) for e in both]
    gb = [stack(e, 1) for e in both]
    ks = [normalize(stack(e, 2), kg[e]) for e in both]
    vb = [stack(e, 3) for e in both]
    cross = lambda e, t: jnp.concatenate(
        [rows_of(b, 4 * e + t + 2 * i) for b in crossed for i in range(2)], axis=0
    )
    kf = [normalize(cross(e, 0), kg[e]) for e in both]
    vf = [cross(e, 1) for e in both]
    kx = normalize(jnp.concatenate([rows_of(late[i], 6) for i in order[1]], axis=0), kg[1])
    vx = jnp.concatenate([rows_of(late[i], 7) for i in order[1]], axis=0)
    far = slice(0, 2 * TILE)
    tiles = [slice(i * TILE, (i + 1) * TILE) for i in range(4)]

    s_own = [dot_nt(qs[e][2], ks[e][2]) for e in both]
    s_far = [dot_nt(qs[e][2][far], kf[e][2]) + far_bias for e in both]
    s_x = jnp.concatenate([dot_nt(qs[1][2][t], kx[2][t]) for t in tiles], axis=0)
    d_own = [dot_nt(gb[e], vb[e]) for e in both]
    d_far = [dot_nt(gb[e][far], vf[e]) for e in both]
    d_x = jnp.concatenate([dot_nt(gb[1][t], vx[t]) for t in tiles], axis=0)
    count = []
    for e in both:
        rows = []
        for a in range(4):
            value = jnp.zeros((TILE, 4 * TILE), F32)
            for b in range(4):
                if a == b:
                    here = jnp.where(lower, 3.0 if a < 2 else 2.0, 0.0)
                else:
                    earlier = (zl ^ order[e][b]) < (zl ^ order[e][a])
                    here = jnp.where(earlier, 2.0 if a < 2 and b < 2 else 1.0, 0.0)
                value = jnp.where(block == b, here, value)
            rows.append(value)
        count.append(jnp.concatenate(rows, axis=0))
    s_own = [jnp.where(count[e] > 0.0, s_own[e], NEG) for e in both]
    peak = lambda x: jnp.max(x, axis=1, keepdims=True)
    add = lambda x: jnp.sum(x, axis=1, keepdims=True)
    top = [peak(x) for x in s_own]
    top[1] = jnp.maximum(top[1], peak(s_x))
    top_far = [jnp.maximum(top[e][far], peak(s_far[e])) for e in both]
    top = [jnp.concatenate([top_far[e], top[e][2 * TILE :]], axis=0) for e in both]
    p_own = [count[e] * jnp.exp2((s_own[e] - top[e]) * LOG_SCALE) for e in both]
    p_far = [jnp.exp2((s_far[e] - top_far[e]) * LOG_SCALE) for e in both]
    p_x = jnp.exp2((s_x - top[1]) * LOG_SCALE)
    total = [add(x) for x in p_own]
    total[1] = total[1] + add(p_x)
    total_far = [add(x) for x in p_far]
    total = [
        jnp.concatenate([total[e][far] + total_far[e], total[e][2 * TILE :]], axis=0) for e in both
    ]
    scale = [1.0 / x for x in total]
    p_own = [p_own[e] * scale[e] for e in both]
    p_far = [p_far[e] * scale[e][far] for e in both]
    p_x = p_x * scale[1]
    w_own = [x.astype(BF) for x in p_own]
    w_far = [x.astype(BF) for x in p_far]
    w_x = p_x.astype(BF)
    rd = [add(w_own[e].astype(F32) * d_own[e]) for e in both]
    rd[1] = rd[1] + add(w_x.astype(F32) * d_x)
    rd_far = [add(w_far[e].astype(F32) * d_far[e]) for e in both]
    rd = [jnp.concatenate([rd[e][far] + rd_far[e], rd[e][2 * TILE :]], axis=0) for e in both]
    ds_far = [(p_far[e] * (d_far[e] - rd[e][far])).astype(BF) for e in both]
    ds_own = [(p_own[e] * (d_own[e] - rd[e])).astype(BF) for e in both]
    ds_x = (p_x * (d_x - rd[1])).astype(BF)

    dk_far = [dot_tn(ds_far[e], qs[e][2][far]) * SCALE for e in both]
    dv_far = [dot_tn(w_far[e], gb[e][far]) for e in both]
    for e in both:
        for m in range(3):
            rows = slice(m * 128, (m + 1) * 128)
            terms[m][256 * e : 256 * e + 128, :] = dk_far[e][rows].astype(BF)
            terms[m][256 * e + 128 : 256 * e + 256, :] = dv_far[e][rows].astype(BF)
    dq = [dot_nn(ds_own[e], ks[e][2]) for e in both]
    dq_far = [dot_nn(ds_far[e], kf[e][2]) for e in both]
    dq_x = jnp.concatenate([dot_nn(ds_x[t], kx[2][t]) for t in tiles], axis=0)
    dq[1] = dq[1] + dq_x
    dq = [
        jnp.concatenate([dq[e][far] + dq_far[e], dq[e][2 * TILE :]], axis=0) * SCALE for e in both
    ]
    dk = [dot_tn(ds_own[e], qs[e][2]) * SCALE for e in both]
    dv = [dot_tn(w_own[e], gb[e]) for e in both]
    dk_x = [dot_tn(ds_x[t], qs[1][2][t]) * SCALE for t in tiles]
    dv_x = [dot_tn(w_x[t], gb[1][t]) for t in tiles]
    gq = [norm_grad(dq[e], qs[e][0], qs[e][1], qg[e]) for e in both]
    down = lambda x: jnp.sum(x, axis=0, keepdims=True)
    for e in both:
        for a, i in enumerate(order[e]):
            out = returned[i]
            if a < 2:
                out[0:TILE, :] = gq[e][tiles[a]]
                far_k[i] = dk[e][tiles[a]]
                far_v[i] = dv[e][tiles[a]]
            else:
                out[TILE : 2 * TILE, :] = gq[e][tiles[a]]
                out[2 * TILE : 3 * TILE, :] = dk[e][tiles[a]].astype(BF)
                out[3 * TILE : 4 * TILE, :] = dv[e][tiles[a]].astype(BF)
            if e == 1:
                out[4 * TILE : 5 * TILE, :] = dk_x[a].astype(BF)
                out[5 * TILE : 6 * TILE, :] = dv_x[a].astype(BF)
        key_sum = down(dk[e] * ks[e][0]) + down(dk_far[e] * kf[e][0])
        if e == 1:
            key_sum += sum(down(dk_x[a] * kx[0][tiles[a]]) for a in range(4))
        gains[pl.ds(heads[e], 1), :] += down(dq[e] * qs[e][0])
        gains[pl.ds(HEADS + heads[e], 1), :] += key_sum
    high, low = split_gains(gains[...])
    for out in (*terms, gains_out):
        at = out.shape[0] - 64
        out[at : at + 32, :] = high
        out[at + 32 :, :] = low


def return_pack_kernel(far_k, far_v, own, u1, u2, u3, y0, y1, y2, y3):
    total = (joined_gains(own) + joined_gains(u2)) + (joined_gains(u1) + joined_gains(u3))
    high, low = split_gains(total)
    for i, y in enumerate((y0, y1, y2, y3)):
        at = 256 * (i & 1) + 64 * (i >> 1)
        dk = far_k[i]
        dv = far_v[i]
        for u in (u1, u2, u3):
            dk += u[at : at + TILE, :].astype(F32)
            dv += u[at + 128 : at + 128 + TILE, :].astype(F32)
        y[0:TILE, :] = dk.astype(BF)
        y[TILE : 2 * TILE, :] = dv.astype(BF)
        y[2 * TILE : 2 * TILE + 32, :] = high
        y[2 * TILE + 32 :, :] = low


def gains_kernel(y0, y2, y3, y1, out):
    out[...] = (joined_gains(y0) + joined_gains(y1)) + (joined_gains(y2) + joined_gains(y3))


def final_kernel(
    c_ref, z0, z2, z3, z1, y0, y2, y3, y1, f0, f1, f2, f3, m0, m1, m2, m3,
    low_k, low_v, high_k, high_v, k_gain, gq_in, gk_in, gv_in,
    gq_out, gk_out, gv_out, done_k, done_v, sems,
):
    c = c_ref[0]
    core, zl, zh, xh = place(c)
    rank = zl ^ (2 * zh)
    copies = []

    def send(src, dst, e, h, n):
        copy = pltpu.make_async_copy(
            src, dst.at[pl.ds(e * TILE, TILE), pl.ds(pl.multiple_of(h * HD, HD), HD)], sems.at[n]
        )
        copy.start()
        copies.append(copy)

    def tile_of(ref, t):
        return ref[t * TILE : (t + 1) * TILE, :]

    jobs = []
    for step in range(4):
        heads = owned_heads(c, step)
        far = step & 1
        near = 1 - far
        y = (y0, y1, y2, y3)[step]
        z = (z0, z1, z2, z3)[step]
        f = (f0, f1, f2, f3)[step]
        m = (m0, m1, m2, m3)[step]
        send(y.at[pl.ds(0, TILE), :], gq_out, far, heads[far], 8 * step)
        send(y.at[pl.ds(TILE, TILE), :], gq_out, near, heads[near], 8 * step + 1)
        owner = rank ^ step
        for i, (h, e, back, at, raw) in enumerate((
            (heads[far], far, z, 0, tile_of(f, 0)),
            (heads[near], near, y, 2, tile_of(m, 4)),
            (heads[1], 0, y, 4, tile_of(m, 6)),
        )):
            part = 3 * (owner & 1) + (far, near, 2)[i]
            jobs.append((3 * step + i, 8 * step + 2 + 2 * i, part, owner < 2, h, e, back, at, raw))
    for n, sem, part, is_low, h, e, back, at, raw in jobs:
        dv = jnp.where(is_low, low_v[part], high_v[part])
        done_v[n] = (dv + tile_of(back, at + 1).astype(F32)).astype(BF)
        send(done_v.at[n], gv_out, e, h, sem + 1)
    kg = [k_gain[pl.ds(job[4], 1), :] for job in jobs]
    ks = [normalize(job[8], x) for job, x in zip(jobs, kg)]
    dk = [
        jnp.where(is_low, low_k[part], high_k[part]) + tile_of(back, at).astype(F32)
        for n, sem, part, is_low, h, e, back, at, raw in jobs
    ]
    done = [norm_grad(x, y[0], y[1], z) for x, y, z in zip(dk, ks, kg)]
    for (n, sem, part, is_low, h, e, back, at, raw), x in zip(jobs, done):
        done_k[n] = x
        send(done_k.at[n], gk_out, e, h, sem)
    for copy in copies:
        copy.wait()


def per_device(q_raw, k_raw, values, d_out, q_gain, k_gain):
    ctx_count = lax.axis_size("ctx")
    dp_count = lax.axis_size("dp")
    here = lax.axis_index("ctx").astype(jnp.int32).reshape(1)
    flat = lambda a: a.reshape(ROWS, HEADS * HD)
    q, k, v, g = (
        pltpu.with_memory_space_constraint(flat(a), pltpu.HBM) for a in (q_raw, k_raw, values, d_out)
    )
    qg = q_gain.reshape(HEADS, HD)
    kg = k_gain.reshape(HEADS, HD)
    params = pltpu.CompilerParams(vmem_limit_bytes=48 * 1024 * 1024)
    shape = jax.ShapeDtypeStruct

    def swap(block, axis, mask):
        count = ctx_count if axis == "ctx" else dp_count
        return lax.ppermute(block, axis, [(i, i ^ mask) for i in range(count)])

    steps = (16, 12, 28)

    def by_distance(blocks):
        return [blocks[i] for i in (0, 2, 3, 1)]

    def around(blocks):
        moved = {i: swap(blocks[i], "ctx", 2 * i) for i in (2, 3, 1)}
        return [blocks[0], moved[1], moved[2], moved[3]]

    def pack_call(early, *after):
        count = 2 if early else 8
        return pl.pallas_call(
            functools.partial(pack_kernel, early),
            in_specs=[smem_spec()] + [hbm_spec()] * 4 + [any_spec()] * len(after),
            out_specs=[any_spec()] * 4,
            out_shape=[shape((count * TILE, HD), BF)] * 4,
            scratch_shapes=[pltpu.SemaphoreType.DMA((4 * count,))],
            compiler_params=params,
            name="pack_early" if early else "pack_late",
        )(here, q, k, v, g, *after)

    packed_early = pack_call(True)
    early = around(packed_early)
    packed_late = pack_call(False, early[1])
    late = around(packed_late)

    def home_call(half, earlier):
        return pl.pallas_call(
            functools.partial(home_kernel, half),
            in_specs=[smem_spec()] + [hbm_spec()] * 4 + [vmem_spec()] * 2 + [hbm_spec()] * len(earlier),
            out_specs=[hbm_spec()] * 3 + [vmem_spec()] * 3,
            out_shape=[shape((ROWS, HEADS * HD), BF)] * 3
            + [shape((6, TILE, HD), F32)] * 2
            + [shape((HEADS, HD), F32)],
            scratch_shapes=[
                pltpu.VMEM((4, ROWS, HEADS * HD // 2), BF),
                pltpu.VMEM((3, ROWS, HEADS * HD // 2), BF),
                pltpu.VMEM((HEADS // 2, ROWS, HD), F32),
                pltpu.VMEM((HEADS // 2, ROWS, HD), F32),
                pltpu.SemaphoreType.DMA((2, 4)),
                pltpu.SemaphoreType.DMA((2, 3)),
            ],
            input_output_aliases={7 + i: i for i in range(len(earlier))},
            compiler_params=params,
            name="home_slab_high" if half else "home_slab_low",
        )(here, q, k, v, g, qg, kg, *earlier)

    low = home_call(0, ())
    high = home_call(1, low[:3])

    onward = pl.pallas_call(
        forward_pack_kernel,
        in_specs=[any_spec()] * 4,
        out_specs=any_spec(),
        out_shape=shape((8 * TILE, HD), BF),
        scratch_shapes=[pltpu.SemaphoreType.DMA((4,))],
        compiler_params=params,
        name="pack_far_rows",
    )(*by_distance(early))
    moved = {mask: swap(onward, "ctx", mask) for mask in (16, 12, 28)}
    crossed = [moved[mask] for mask in steps]

    outs = pl.pallas_call(
        owner_kernel,
        in_specs=[smem_spec()] + [vmem_spec()] * 15,
        out_specs=[vmem_spec()] * 10,
        out_shape=[shape((6 * TILE, HD), BF)] * 4
        + [shape((9 * TILE, HD), BF)] * 3
        + [shape((4, TILE, HD), F32)] * 2
        + [shape((TILE, HD), BF)],
        scratch_shapes=[pltpu.VMEM((2 * HEADS, HD), F32)],
        compiler_params=params,
        name="owned_heads",
    )(here, *by_distance(early), *by_distance(late), *crossed, qg, kg, low[5], high[5])
    back_early, terms, far_k, far_v, own_gains = outs[:4], outs[4:7], outs[7], outs[8], outs[9]
    moved = {mask: swap(terms[steps.index(mask)], "ctx", mask) for mask in (28, 12, 16)}
    terms_in = [moved[mask] for mask in steps]

    def pair_sum(x, axis, mask):
        return x + swap(x, axis, mask)

    def quad_sum(x, axis, mask):
        one, two, three = (swap(x, axis, i * mask) for i in (1, 2, 3))
        return (x + one) + (two + three)

    back_late = pl.pallas_call(
        return_pack_kernel,
        in_specs=[vmem_spec()] * 6,
        out_specs=[vmem_spec()] * 4,
        out_shape=[shape((3 * TILE, HD), BF)] * 4,
        compiler_params=params,
        name="add_far_terms",
    )(far_k, far_v, own_gains, *terms_in[::-1])
    home_early = around(back_early)
    home_late = around(back_late)

    gains = pl.pallas_call(
        gains_kernel,
        in_specs=[vmem_spec()] * 4,
        out_specs=vmem_spec(),
        out_shape=shape((2 * HEADS, HD), F32),
        compiler_params=params,
        name="sum_gains",
    )(*by_distance(home_late))
    gains = quad_sum(gains, "dp", 1)
    gains = pair_sum(gains, "dp", 4)
    gains = pair_sum(gains, "ctx", 1)

    gq, gk, gv = pl.pallas_call(
        final_kernel,
        in_specs=[smem_spec()] + [vmem_spec()] * 21 + [any_spec()] * 3,
        out_specs=[any_spec()] * 3,
        out_shape=[shape((ROWS, HEADS * HD), BF)] * 3,
        scratch_shapes=[pltpu.VMEM((12, TILE, HD), BF)] * 2 + [pltpu.SemaphoreType.DMA((32,))],
        input_output_aliases={22: 0, 23: 1, 24: 2},
        compiler_params=params,
        name="finish_rows",
    )(
        here, *by_distance(home_late), *by_distance(home_early), *packed_early, *packed_late,
        low[3], low[4], high[3], high[4], kg, *high[:3],
    )
    whole = lambda a: a.reshape(1, ROWS, HEADS * HD)
    return (
        whole(gq),
        whole(gk),
        whole(gv),
        gains[:HEADS].reshape(HEADS * HD),
        gains[HEADS:].reshape(HEADS * HD),
    )


def solution(mesh):
    rows = P("dp", "ctx", None)
    return jax.shard_map(
        per_device,
        mesh=mesh,
        in_specs=(rows, rows, rows, rows, P(), P()),
        out_specs=(rows, rows, rows, P(), P()),
        check_vma=False,
    )
```

```python
import functools

import jax
import jax.numpy as jnp
from jax import lax
from jax.experimental import pallas as pl
from jax.experimental.pallas import tpu as pltpu
from jax.sharding import PartitionSpec as P

HEADS = 16
HD = 128
TILE = 64
ROWS = 128
EPS = 1e-06
SCALE = HD ** (-0.5)
BF = jnp.bfloat16
F32 = jnp.float32
NEG = -jnp.inf
LOG_SCALE = SCALE * 1.4426950408889634


def vmem_spec():
    return pl.BlockSpec(memory_space=pltpu.VMEM)


def smem_spec():
    return pl.BlockSpec(memory_space=pltpu.SMEM)


def hbm_spec():
    return pl.BlockSpec(memory_space=pltpu.HBM)


def any_spec():
    return pl.BlockSpec(memory_space=pl.ANY)


def place(c):
    core = c & 1
    zl = (c >> 1) & 3
    zh = (c >> 3) & 1
    xh = (c >> 4) & 1
    return core, zl, zh, xh


def owned_heads(c, k):
    core, zl, zh, xh = place(c)
    rank = (zl ^ (2 * zh)) ^ k
    par = rank & 1
    base = 2 * core + 8 * (rank >> 1)
    return base + 4 * par, base + 1 + 4 * (1 - par)


def normalize(raw, gain):
    x = raw.astype(F32)
    inverse = lax.rsqrt(jnp.mean(x * x, axis=-1, keepdims=True) + EPS)
    normed = x * inverse
    return normed, inverse, (normed * gain).astype(BF)


def norm_grad(upstream, normed, inverse, gain):
    weighted = upstream * gain
    inner = jnp.mean(weighted * normed, axis=-1, keepdims=True)
    return (inverse * (weighted - normed * inner)).astype(BF)


def dot_nt(a, b):
    return lax.dot_general(a, b, (((1,), (1,)), ((), ())), preferred_element_type=F32)


def dot_nn(a, b):
    return lax.dot_general(a, b, (((1,), (0,)), ((), ())), preferred_element_type=F32)


def dot_tn(a, b):
    return lax.dot_general(a, b, (((0,), (0,)), ((), ())), preferred_element_type=F32)


def early_tiles(step):
    far = step & 1
    tiles = (("k", far), ("v", far))
    return tiles + late_tiles(step) if step == 1 else tiles


def late_tiles(step):
    far = step & 1
    near = 1 - far
    return (("q", far), ("g", far), ("q", near), ("g", near), ("k", near), ("v", near), ("k", 2), ("v", 2))


def pack_kernel(plan, c_ref, q, k, v, g, *refs):
    outs, sems = refs[-1 - len(plan) : -1], refs[-1]
    sources = {"q": q, "k": k, "v": v, "g": g}
    c = c_ref[0]
    copies = []
    for (step, tiles), out in zip(plan, outs):
        heads = owned_heads(c, step)
        for t, (name, e) in enumerate(tiles):
            row = 0 if e == 2 else e * TILE
            h = heads[min(e, 1)]
            copy = pltpu.make_async_copy(
                sources[name].at[pl.ds(row, TILE), pl.ds(pl.multiple_of(h * HD, HD), HD)],
                out.at[pl.ds(t * TILE, TILE), :],
                sems.at[len(copies)],
            )
            copy.start()
            copies.append(copy)
    for copy in copies:
        copy.wait()


def split_gains(total):
    high = total.astype(BF)
    return high, (total - high.astype(F32)).astype(BF)


def joined_gains(ref):
    at = ref.shape[0] - 64
    return ref[at : at + 32, :].astype(F32) + ref[at + 32 : at + 64, :].astype(F32)


def forward_pack_kernel(f0, f2, f3, f1, ready, out, sems):
    copies = []
    for k, src in enumerate((f0, f2, f1, f3)):
        copy = pltpu.make_async_copy(
            src.at[pl.ds(0, 2 * TILE), :], out.at[pl.ds(2 * k * TILE, 2 * TILE), :], sems.at[k]
        )
        copy.start()
        copies.append(copy)
    for copy in copies:
        copy.wait()


def home_kernel(
    c_ref, q, k, v, g, q_gain, k_gain, gq_out, gk_out, gv_out, part_k, part_v, gains,
    loads, stores, dk_all, dv_all, in_sems, out_sems,
):
    outs = (gq_out, gk_out, gv_out)
    c = c_ref[0]
    core = c & 1
    count = HEADS
    group = 8
    first = 0
    for n in range(count // group):
        cols = pl.ds((first + n * group) * HD, group * HD)
        for i, src in enumerate((q, k, v, g)):
            pltpu.make_async_copy(
                src.at[:, cols], loads.at[i, :, pl.ds(n * group * HD, group * HD)], in_sems.at[n, i]
            ).start()
    row = lax.broadcasted_iota(jnp.int32, (ROWS, ROWS), 0)
    col = lax.broadcasted_iota(jnp.int32, (ROWS, ROWS), 1)
    causal = col <= row
    tile_of_row = lax.broadcasted_iota(jnp.int32, (ROWS, 1), 0) // TILE
    copies = []
    for n in range(count // group):
        cols = pl.ds((first + n * group) * HD, group * HD)
        here = pl.ds(n * group * HD, group * HD)
        for i, src in enumerate((q, k, v, g)):
            pltpu.make_async_copy(src.at[:, cols], loads.at[i, :, here], in_sems.at[n, i]).wait()
        locs = [n * group + i for i in range(group)]
        spans = [slice(l * HD, (l + 1) * HD) for l in locs]
        qg = [q_gain[first + l : first + l + 1, :] for l in locs]
        kg = [k_gain[first + l : first + l + 1, :] for l in locs]
        qs = [normalize(loads[0, :, sp], x) for sp, x in zip(spans, qg)]
        ks = [normalize(loads[1, :, sp], x) for sp, x in zip(spans, kg)]
        vb = [loads[2, :, sp] for sp in spans]
        gb = [loads[3, :, sp] for sp in spans]
        s = [jnp.where(causal, dot_nt(x[2], y[2]), NEG) for x, y in zip(qs, ks)]
        dp = [dot_nt(x, y) for x, y in zip(gb, vb)]
        top = [jnp.max(x, axis=1, keepdims=True) for x in s]
        p = [jnp.exp2((x - t) * LOG_SCALE) for x, t in zip(s, top)]
        total = [jnp.sum(x, axis=1, keepdims=True) for x in p]
        keep = []
        for l in locs:
            kind = (first + l) % 4
            owned = (tile_of_row == (kind & 1)) & (core == (kind >> 1))
            keep.append(jnp.where(owned, 0.0, 1.0))
        p = [x * (z / t) for x, z, t in zip(p, keep, total)]
        w = [x.astype(BF) for x in p]
        rd = [jnp.sum(x.astype(F32) * y, axis=1, keepdims=True) for x, y in zip(w, dp)]
        ds = [(x * (y - z)).astype(BF) for x, y, z in zip(p, dp, rd)]
        dq = [dot_nn(x, y[2]) * SCALE for x, y in zip(ds, ks)]
        dk = [dot_tn(x, y[2]) * SCALE for x, y in zip(ds, qs)]
        dv = [dot_tn(x, y) for x, y in zip(w, gb)]
        for i, (l, sp) in enumerate(zip(locs, spans)):
            stores[0, :, sp] = norm_grad(dq[i], qs[i][0], qs[i][1], qg[i])
            stores[1, :, sp] = norm_grad(dk[i], ks[i][0], ks[i][1], kg[i])
            stores[2, :, sp] = dv[i].astype(BF)
            dk_all[l] = dk[i]
            dv_all[l] = dv[i]
            gains[l : l + 1, :] = jnp.sum(dq[i] * qs[i][0], axis=0, keepdims=True)
            gains[count + l : count + l + 1, :] = jnp.sum(dk[i] * ks[i][0], axis=0, keepdims=True)
        for i, dst in enumerate(outs):
            copy = pltpu.make_async_copy(stores.at[i, :, here], dst.at[:, cols], out_sems.at[n, i])
            copy.start()
            copies.append(copy)
    for j in range(4):
        h0 = 2 * core + 8 * (j >> 1) + 4 * (j & 1)
        h1 = 2 * core + 1 + 8 * (j >> 1) + 4 * (1 - (j & 1))
        for i, (h, e) in enumerate(((h0, 0), (h1, 1), (h1, 0))):
            rows = slice(e * TILE, (e + 1) * TILE)
            part_k[3 * j + i] = dk_all[h, rows, :]
            part_v[3 * j + i] = dv_all[h, rows, :]
    for copy in copies:
        copy.wait()


def owner_kernel(
    c_ref, f0, f2, f3, f1, r0, r2, r3, b3, b2, b1, q_gain, k_gain, home_gains,
    x0, x1, x2, x3, t1, t2, t3, far_k, far_v, gains_out, gains,
):
    c = c_ref[0]
    core, zl, zh, xh = place(c)
    heads = owned_heads(c, 0)
    early = (f0, f1, f2, f3)
    late = (r0, f1.at[pl.ds(2 * TILE, 8 * TILE), :], r2, r3)
    crossed = (b1, b2, b3)
    returned = (x0, x1, x2, x3)
    terms = (t1, t2, t3)
    live = (xh == 1, zh == 1, xh == 1)
    gains[...] = home_gains[...]
    row = lax.broadcasted_iota(jnp.int32, (TILE, 4 * TILE), 0)
    col = lax.broadcasted_iota(jnp.int32, (TILE, 4 * TILE), 1)
    block = col >> 6
    lower = (col & (TILE - 1)) <= row
    far_block = lax.broadcasted_iota(jnp.int32, (1, 6 * TILE), 1) >> 7
    bias = [jnp.where(x, 0.0, NEG) for x in live]
    far_bias = jnp.where(far_block == 0, bias[0], jnp.where(far_block == 1, bias[1], bias[2]))

    def rows_of(ref, tile):
        return ref[tile * TILE : (tile + 1) * TILE, :]

    both = (0, 1)
    order = ((0, 2, 1, 3), (1, 3, 0, 2))
    qg = [q_gain[pl.ds(h, 1), :] for h in heads]
    kg = [k_gain[pl.ds(h, 1), :] for h in heads]


    def stack(e, t):
        parts = []
        for a, i in enumerate(order[e]):
            if a < 2:
                parts.append(rows_of(late[i], t) if t < 2 else rows_of(early[i], t - 2))
            else:
                parts.append(rows_of(late[i], 2 + t))
        return jnp.concatenate(parts, axis=0)

    qs = [normalize(stack(e, 0), qg[e]) for e in both]
    gb = [stack(e, 1) for e in both]
    ks = [normalize(stack(e, 2), kg[e]) for e in both]
    vb = [stack(e, 3) for e in both]
    cross = lambda e, t: jnp.concatenate(
        [rows_of(b, 4 * e + t + 2 * i) for b in crossed for i in range(2)], axis=0
    )
    kf = [normalize(cross(e, 0), kg[e]) for e in both]
    vf = [cross(e, 1) for e in both]
    kx = normalize(jnp.concatenate([rows_of(late[i], 6) for i in order[1]], axis=0), kg[1])
    vx = jnp.concatenate([rows_of(late[i], 7) for i in order[1]], axis=0)
    far = slice(0, 2 * TILE)
    tiles = [slice(i * TILE, (i + 1) * TILE) for i in range(4)]

    s_own = [dot_nt(qs[e][2], ks[e][2]) for e in both]
    s_far = [dot_nt(qs[e][2][far], kf[e][2]) + far_bias for e in both]
    s_x = jnp.concatenate([dot_nt(qs[1][2][t], kx[2][t]) for t in tiles], axis=0)
    d_own = [dot_nt(gb[e], vb[e]) for e in both]
    d_far = [dot_nt(gb[e][far], vf[e]) for e in both]
    d_x = jnp.concatenate([dot_nt(gb[1][t], vx[t]) for t in tiles], axis=0)
    count = []
    for e in both:
        rows = []
        for a in range(4):
            value = jnp.zeros((TILE, 4 * TILE), F32)
            for b in range(4):
                if a == b:
                    here = jnp.where(lower, 3.0 if a < 2 else 2.0, 0.0)
                else:
                    earlier = (zl ^ order[e][b]) < (zl ^ order[e][a])
                    here = jnp.where(earlier, 2.0 if a < 2 and b < 2 else 1.0, 0.0)
                value = jnp.where(block == b, here, value)
            rows.append(value)
        count.append(jnp.concatenate(rows, axis=0))
    s_own = [jnp.where(count[e] > 0.0, s_own[e], NEG) for e in both]
    peak = lambda x: jnp.max(x, axis=1, keepdims=True)
    add = lambda x: jnp.sum(x, axis=1, keepdims=True)
    top = [peak(x) for x in s_own]
    top[1] = jnp.maximum(top[1], peak(s_x))
    top_far = [jnp.maximum(top[e][far], peak(s_far[e])) for e in both]
    top = [jnp.concatenate([top_far[e], top[e][2 * TILE :]], axis=0) for e in both]
    p_own = [count[e] * jnp.exp2((s_own[e] - top[e]) * LOG_SCALE) for e in both]
    p_far = [jnp.exp2((s_far[e] - top_far[e]) * LOG_SCALE) for e in both]
    p_x = jnp.exp2((s_x - top[1]) * LOG_SCALE)
    total = [add(x) for x in p_own]
    total[1] = total[1] + add(p_x)
    total_far = [add(x) for x in p_far]
    total = [
        jnp.concatenate([total[e][far] + total_far[e], total[e][2 * TILE :]], axis=0) for e in both
    ]
    scale = [1.0 / x for x in total]
    p_own = [p_own[e] * scale[e] for e in both]
    p_far = [p_far[e] * scale[e][far] for e in both]
    p_x = p_x * scale[1]
    w_own = [x.astype(BF) for x in p_own]
    w_far = [x.astype(BF) for x in p_far]
    w_x = p_x.astype(BF)
    rd = [add(w_own[e].astype(F32) * d_own[e]) for e in both]
    rd[1] = rd[1] + add(w_x.astype(F32) * d_x)
    rd_far = [add(w_far[e].astype(F32) * d_far[e]) for e in both]
    rd = [jnp.concatenate([rd[e][far] + rd_far[e], rd[e][2 * TILE :]], axis=0) for e in both]
    ds_far = [(p_far[e] * (d_far[e] - rd[e][far])).astype(BF) for e in both]
    ds_own = [(p_own[e] * (d_own[e] - rd[e])).astype(BF) for e in both]
    ds_x = (p_x * (d_x - rd[1])).astype(BF)

    dk_far = [dot_tn(ds_far[e], qs[e][2][far]) * SCALE for e in both]
    dv_far = [dot_tn(w_far[e], gb[e][far]) for e in both]
    for e in both:
        for m in range(3):
            rows = slice(m * 128, (m + 1) * 128)
            terms[m][256 * e : 256 * e + 128, :] = dk_far[e][rows].astype(BF)
            terms[m][256 * e + 128 : 256 * e + 256, :] = dv_far[e][rows].astype(BF)
    dq = [dot_nn(ds_own[e], ks[e][2]) for e in both]
    dq_far = [dot_nn(ds_far[e], kf[e][2]) for e in both]
    dq_x = jnp.concatenate([dot_nn(ds_x[t], kx[2][t]) for t in tiles], axis=0)
    dq[1] = dq[1] + dq_x
    dq = [
        jnp.concatenate([dq[e][far] + dq_far[e], dq[e][2 * TILE :]], axis=0) * SCALE for e in both
    ]
    dk = [dot_tn(ds_own[e], qs[e][2]) * SCALE for e in both]
    dv = [dot_tn(w_own[e], gb[e]) for e in both]
    dk_x = [dot_tn(ds_x[t], qs[1][2][t]) * SCALE for t in tiles]
    dv_x = [dot_tn(w_x[t], gb[1][t]) for t in tiles]
    gq = [norm_grad(dq[e], qs[e][0], qs[e][1], qg[e]) for e in both]
    down = lambda x: jnp.sum(x, axis=0, keepdims=True)
    for e in both:
        for a, i in enumerate(order[e]):
            out = returned[i]
            if a < 2:
                out[0:TILE, :] = gq[e][tiles[a]]
                far_k[i] = dk[e][tiles[a]]
                far_v[i] = dv[e][tiles[a]]
            else:
                out[TILE : 2 * TILE, :] = gq[e][tiles[a]]
                out[2 * TILE : 3 * TILE, :] = dk[e][tiles[a]].astype(BF)
                out[3 * TILE : 4 * TILE, :] = dv[e][tiles[a]].astype(BF)
            if e == 1:
                out[4 * TILE : 5 * TILE, :] = dk_x[a].astype(BF)
                out[5 * TILE : 6 * TILE, :] = dv_x[a].astype(BF)
        key_sum = down(dk[e] * ks[e][0]) + down(dk_far[e] * kf[e][0])
        if e == 1:
            key_sum += sum(down(dk_x[a] * kx[0][tiles[a]]) for a in range(4))
        gains[pl.ds(heads[e], 1), :] += down(dq[e] * qs[e][0])
        gains[pl.ds(HEADS + heads[e], 1), :] += key_sum
    high, low = split_gains(gains[...])
    for out in (*terms, gains_out):
        at = out.shape[0] - 64
        out[at : at + 32, :] = high
        out[at + 32 :, :] = low


def return_pack_kernel(far_k, far_v, own, u1, u2, u3, x1, *refs):
    y0, y1, y2, y3 = refs[-4:]
    total = (joined_gains(own) + joined_gains(u2)) + (joined_gains(u1) + joined_gains(u3))
    high, low = split_gains(total)
    for i, y in enumerate((y0, y1, y2, y3)):
        at = 256 * (i & 1) + 64 * (i >> 1)
        dk = far_k[i]
        dv = far_v[i]
        for u in (u1, u2, u3):
            dk += u[at : at + TILE, :].astype(F32)
            dv += u[at + 128 : at + 128 + TILE, :].astype(F32)
        y[0:TILE, :] = dk.astype(BF)
        y[TILE : 2 * TILE, :] = dv.astype(BF)
        at = y.shape[0] - 64
        y[at : at + 32, :] = high
        y[at + 32 :, :] = low
    y1[2 * TILE : 8 * TILE, :] = x1[...]


def gains_kernel(y0, y2, y3, y1, out):
    out[...] = (joined_gains(y0) + joined_gains(y1)) + (joined_gains(y2) + joined_gains(y3))


def last_sum_kernel(mine, other, q_out, k_out):
    q_out[...] = mine[0:HEADS, :] + other[0:HEADS, :]
    k_out[...] = mine[HEADS:, :] + other[HEADS:, :]


def final_kernel(
    c_ref, z0, z2, z3, z1, y0, y2, y3, f0, f1, f2, f3, m0, m2, m3,
    part_k, part_v, k_gain, gq_in, gk_in, gv_in,
    gq_out, gk_out, gv_out, done_k, done_v, sems,
):
    c = c_ref[0]
    core, zl, zh, xh = place(c)
    rank = zl ^ (2 * zh)
    copies = []

    def send(src, dst, e, h, n):
        copy = pltpu.make_async_copy(
            src, dst.at[pl.ds(e * TILE, TILE), pl.ds(pl.multiple_of(h * HD, HD), HD)], sems.at[n]
        )
        copy.start()
        copies.append(copy)

    def tile_of(ref, t):
        return ref[t * TILE : (t + 1) * TILE, :]

    y1 = z1.at[pl.ds(2 * TILE, 6 * TILE), :]
    m1 = f1.at[pl.ds(2 * TILE, 8 * TILE), :]
    jobs = []
    for step in range(4):
        heads = owned_heads(c, step)
        far = step & 1
        near = 1 - far
        y = (y0, y1, y2, y3)[step]
        z = (z0, z1, z2, z3)[step]
        f = (f0, f1, f2, f3)[step]
        m = (m0, m1, m2, m3)[step]
        send(y.at[pl.ds(0, TILE), :], gq_out, far, heads[far], 8 * step)
        send(y.at[pl.ds(TILE, TILE), :], gq_out, near, heads[near], 8 * step + 1)
        owner = rank ^ step
        for i, (h, e, back, at, raw) in enumerate((
            (heads[far], far, z, 0, tile_of(f, 0)),
            (heads[near], near, y, 2, tile_of(m, 4)),
            (heads[1], 0, y, 4, tile_of(m, 6)),
        )):
            part = 3 * owner + (far, near, 2)[i]
            jobs.append((3 * step + i, 8 * step + 2 + 2 * i, part, h, e, back, at, raw))
    for n, sem, part, h, e, back, at, raw in jobs:
        done_v[n] = (part_v[part] + tile_of(back, at + 1).astype(F32)).astype(BF)
        send(done_v.at[n], gv_out, e, h, sem + 1)
    kg = [k_gain[pl.ds(job[3], 1), :] for job in jobs]
    ks = [normalize(job[7], x) for job, x in zip(jobs, kg)]
    dk = [
        part_k[part] + tile_of(back, at).astype(F32)
        for n, sem, part, h, e, back, at, raw in jobs
    ]
    done = [norm_grad(x, y[0], y[1], z) for x, y, z in zip(dk, ks, kg)]
    for (n, sem, part, h, e, back, at, raw), x in zip(jobs, done):
        done_k[n] = x
        send(done_k.at[n], gk_out, e, h, sem)
    for copy in copies:
        copy.wait()


def per_device(q_raw, k_raw, values, d_out, q_gain, k_gain):
    ctx_count = lax.axis_size("ctx")
    dp_count = lax.axis_size("dp")
    here = lax.axis_index("ctx").astype(jnp.int32).reshape(1)
    flat = lambda a: a.reshape(ROWS, HEADS * HD)
    q, k, v, g = (
        pltpu.with_memory_space_constraint(flat(a), pltpu.HBM) for a in (q_raw, k_raw, values, d_out)
    )
    qg = q_gain.reshape(HEADS, HD)
    kg = k_gain.reshape(HEADS, HD)
    params = pltpu.CompilerParams(vmem_limit_bytes=48 * 1024 * 1024)
    shape = jax.ShapeDtypeStruct

    def swap(block, axis, mask):
        count = ctx_count if axis == "ctx" else dp_count
        return lax.ppermute(block, axis, [(i, i ^ mask) for i in range(count)])

    steps = (16, 12, 28)

    def by_distance(blocks):
        return [blocks[i] for i in (0, 2, 3, 1)]

    def around(blocks):
        moved = {i: swap(blocks[i], "ctx", 2 * i) for i in (2, 3, 1)}
        return [blocks[0], moved[1], moved[2], moved[3]]

    def pack_call(name, plan, *after):
        return pl.pallas_call(
            functools.partial(pack_kernel, plan),
            in_specs=[smem_spec()] + [hbm_spec()] * 4 + [any_spec()] * len(after),
            out_specs=[any_spec()] * len(plan),
            out_shape=[shape((len(tiles) * TILE, HD), BF) for _, tiles in plan],
            scratch_shapes=[pltpu.SemaphoreType.DMA((sum(len(tiles) for _, tiles in plan),))],
            compiler_params=params,
            name=name,
        )(here, q, k, v, g, *after)

    packed_early = pack_call("pack_early", tuple((i, early_tiles(i)) for i in range(4)))
    early = around(packed_early)
    packed_late = pack_call("pack_late", tuple((i, late_tiles(i)) for i in (0, 2, 3)), early[1])
    late = [packed_late[0], swap(packed_late[1], "ctx", 4), swap(packed_late[2], "ctx", 6)]

    gq_home, gk_home, gv_home, part_k, part_v, home_gains = pl.pallas_call(
        home_kernel,
        in_specs=[smem_spec()] + [hbm_spec()] * 4 + [vmem_spec()] * 2,
        out_specs=[hbm_spec()] * 3 + [vmem_spec()] * 3,
        out_shape=[shape((ROWS, HEADS * HD), BF)] * 3
        + [shape((12, TILE, HD), F32)] * 2
        + [shape((2 * HEADS, HD), F32)],
        scratch_shapes=[
            pltpu.VMEM((4, ROWS, HEADS * HD), BF),
            pltpu.VMEM((3, ROWS, HEADS * HD), BF),
            pltpu.VMEM((HEADS, ROWS, HD), F32),
            pltpu.VMEM((HEADS, ROWS, HD), F32),
            pltpu.SemaphoreType.DMA((2, 4)),
            pltpu.SemaphoreType.DMA((2, 3)),
        ],
        compiler_params=params,
        name="home_slab",
    )(here, q, k, v, g, qg, kg)

    onward = pl.pallas_call(
        forward_pack_kernel,
        in_specs=[any_spec()] * 5,
        out_specs=any_spec(),
        out_shape=shape((8 * TILE, HD), BF),
        scratch_shapes=[pltpu.SemaphoreType.DMA((4,))],
        compiler_params=params,
        name="pack_far_rows",
    )(*by_distance(early), packed_late[0])
    moved = {mask: swap(onward, "ctx", mask) for mask in (16, 12, 28)}
    crossed = [moved[mask] for mask in steps]

    outs = pl.pallas_call(
        owner_kernel,
        in_specs=[smem_spec()] + [vmem_spec()] * 13,
        out_specs=[vmem_spec()] * 10,
        out_shape=[shape((6 * TILE, HD), BF)] * 4
        + [shape((9 * TILE, HD), BF)] * 3
        + [shape((4, TILE, HD), F32)] * 2
        + [shape((TILE, HD), BF)],
        scratch_shapes=[pltpu.VMEM((2 * HEADS, HD), F32)],
        compiler_params=params,
        name="owned_heads",
    )(here, *by_distance(early), *late, crossed[2], crossed[1], crossed[0], qg, kg, home_gains)
    back_early, terms, far_k, far_v, own_gains = outs[:4], outs[4:7], outs[7], outs[8], outs[9]
    moved = {mask: swap(terms[steps.index(mask)], "ctx", mask) for mask in (28, 12, 16)}
    terms_in = [moved[mask] for mask in steps]

    def pair_sum(x, axis, mask):
        return x + swap(x, axis, mask)

    def quad_sum(x, axis, mask):
        one, two, three = (swap(x, axis, i * mask) for i in (1, 2, 3))
        return (x + one) + (two + three)

    home_early = [back_early[0], swap(back_early[2], "ctx", 4), swap(back_early[3], "ctx", 6)]
    waits = ()
    back_late = pl.pallas_call(
        return_pack_kernel,
        in_specs=[vmem_spec()] * 7 + [any_spec()] * len(waits),
        out_specs=[vmem_spec()] * 4,
        out_shape=[shape((count * TILE, HD), BF) for count in (3, 9, 3, 3)],
        compiler_params=params,
        name="add_far_terms",
    )(far_k, far_v, own_gains, *terms_in[::-1], back_early[1], *waits)
    home_late = around(back_late)

    gains = pl.pallas_call(
        gains_kernel,
        in_specs=[vmem_spec()] * 4,
        out_specs=vmem_spec(),
        out_shape=shape((2 * HEADS, HD), F32),
        compiler_params=params,
        name="sum_gains",
    )(*by_distance(home_late))
    gains = quad_sum(gains, "dp", 1)
    gains = pair_sum(gains, "dp", 4)
    q_sum, k_sum = pl.pallas_call(
        last_sum_kernel,
        in_specs=[vmem_spec()] * 2,
        out_specs=[vmem_spec()] * 2,
        out_shape=[shape((HEADS, HD), F32)] * 2,
        compiler_params=params,
        name="last_sum",
    )(gains, swap(gains, "ctx", 1))

    gq, gk, gv = pl.pallas_call(
        final_kernel,
        in_specs=[smem_spec()] + [vmem_spec()] * 17 + [any_spec()] * 3,
        out_specs=[any_spec()] * 3,
        out_shape=[shape((ROWS, HEADS * HD), BF)] * 3,
        scratch_shapes=[pltpu.VMEM((12, TILE, HD), BF)] * 2 + [pltpu.SemaphoreType.DMA((32,))],
        input_output_aliases={18: 0, 19: 1, 20: 2},
        compiler_params=params,
        name="finish_rows",
    )(
        here, *by_distance(home_late), *home_early, *packed_early, *packed_late,
        part_k, part_v, kg, gq_home, gk_home, gv_home,
    )
    whole = lambda a: a.reshape(1, ROWS, HEADS * HD)
    return (
        whole(gq),
        whole(gk),
        whole(gv),
        q_sum.reshape(HEADS * HD),
        k_sum.reshape(HEADS * HD),
    )


def solution(mesh):
    rows = P("dp", "ctx", None)
    return jax.shard_map(
        per_device,
        mesh=mesh,
        in_specs=(rows, rows, rows, rows, P(), P()),
        out_specs=(rows, rows, rows, P(), P()),
        check_vma=False,
    )
```

```python
import functools

import jax
import jax.numpy as jnp
from jax import lax
from jax.experimental import pallas as pl
from jax.experimental.pallas import tpu as pltpu
from jax.sharding import PartitionSpec as P

HEADS = 16
HD = 128
TILE = 64
ROWS = 128
EPS = 1e-06
SCALE = HD ** (-0.5)
BF = jnp.bfloat16
F32 = jnp.float32
NEG = -jnp.inf
LOG_SCALE = SCALE * 1.4426950408889634


def vmem_spec():
    return pl.BlockSpec(memory_space=pltpu.VMEM)


def smem_spec():
    return pl.BlockSpec(memory_space=pltpu.SMEM)


def hbm_spec():
    return pl.BlockSpec(memory_space=pltpu.HBM)


def any_spec():
    return pl.BlockSpec(memory_space=pl.ANY)


def place(c):
    core = c & 1
    zl = (c >> 1) & 3
    zh = (c >> 3) & 1
    xh = (c >> 4) & 1
    return core, zl, zh, xh


def owned_heads(c, k):
    core, zl, zh, xh = place(c)
    rank = (zl ^ (2 * zh)) ^ k
    par = rank & 1
    base = 2 * core + 8 * (rank >> 1)
    return base + 4 * par, base + 1 + 4 * (1 - par)


def normalize(raw, gain):
    x = raw.astype(F32)
    inverse = lax.rsqrt(jnp.mean(x * x, axis=-1, keepdims=True) + EPS)
    normed = x * inverse
    return normed, inverse, (normed * gain).astype(BF)


def norm_grad(upstream, normed, inverse, gain):
    weighted = upstream * gain
    inner = jnp.mean(weighted * normed, axis=-1, keepdims=True)
    return (inverse * (weighted - normed * inner)).astype(BF)


def dot_nt(a, b):
    return lax.dot_general(a, b, (((1,), (1,)), ((), ())), preferred_element_type=F32)


def dot_nn(a, b):
    return lax.dot_general(a, b, (((1,), (0,)), ((), ())), preferred_element_type=F32)


def dot_tn(a, b):
    return lax.dot_general(a, b, (((0,), (0,)), ((), ())), preferred_element_type=F32)


def early_tiles(step):
    far = step & 1
    tiles = (("k", far), ("v", far))
    return tiles + late_tiles(step) if step == 1 else tiles


def late_tiles(step):
    far = step & 1
    near = 1 - far
    return (("q", far), ("g", far), ("q", near), ("g", near), ("k", near), ("v", near), ("k", 2), ("v", 2))


def pack_kernel(plan, c_ref, q, k, v, g, *refs):
    outs, sems = refs[-1 - len(plan) : -1], refs[-1]
    sources = {"q": q, "k": k, "v": v, "g": g}
    c = c_ref[0]
    copies = []
    for (step, tiles), out in zip(plan, outs):
        heads = owned_heads(c, step)
        for t, (name, e) in enumerate(tiles):
            row = 0 if e == 2 else e * TILE
            h = heads[min(e, 1)]
            copy = pltpu.make_async_copy(
                sources[name].at[pl.ds(row, TILE), pl.ds(pl.multiple_of(h * HD, HD), HD)],
                out.at[pl.ds(t * TILE, TILE), :],
                sems.at[len(copies)],
            )
            copy.start()
            copies.append(copy)
    for copy in copies:
        copy.wait()


def split_gains(total):
    high = total.astype(BF)
    return high, (total - high.astype(F32)).astype(BF)


def joined_gains(ref):
    at = ref.shape[0] - 64
    return ref[at : at + 32, :].astype(F32) + ref[at + 32 : at + 64, :].astype(F32)


def forward_pack_kernel(f0, f3, f2, f1, ready, out, sems):
    copies = []
    for k, src in enumerate((f0, f2, f1, f3)):
        copy = pltpu.make_async_copy(
            src.at[pl.ds(0, 2 * TILE), :], out.at[pl.ds(2 * k * TILE, 2 * TILE), :], sems.at[k]
        )
        copy.start()
        copies.append(copy)
    for copy in copies:
        copy.wait()


def home_kernel(
    c_ref, q, k, v, g, q_gain, k_gain, gq_out, gk_out, gv_out, part_k, part_v, gains,
    loads, stores, dk_all, dv_all, in_sems, out_sems,
):
    outs = (gq_out, gk_out, gv_out)
    c = c_ref[0]
    core = c & 1
    count = HEADS
    group = 8
    first = 0
    for n in range(count // group):
        cols = pl.ds((first + n * group) * HD, group * HD)
        for i, src in enumerate((q, k, v, g)):
            pltpu.make_async_copy(
                src.at[:, cols], loads.at[i, :, pl.ds(n * group * HD, group * HD)], in_sems.at[n, i]
            ).start()
    row = lax.broadcasted_iota(jnp.int32, (ROWS, ROWS), 0)
    col = lax.broadcasted_iota(jnp.int32, (ROWS, ROWS), 1)
    causal = col <= row
    tile_of_row = lax.broadcasted_iota(jnp.int32, (ROWS, 1), 0) // TILE
    copies = []
    for n in range(count // group):
        cols = pl.ds((first + n * group) * HD, group * HD)
        here = pl.ds(n * group * HD, group * HD)
        for i, src in enumerate((q, k, v, g)):
            pltpu.make_async_copy(src.at[:, cols], loads.at[i, :, here], in_sems.at[n, i]).wait()
        locs = [n * group + i for i in range(group)]
        spans = [slice(l * HD, (l + 1) * HD) for l in locs]
        qg = [q_gain[first + l : first + l + 1, :] for l in locs]
        kg = [k_gain[first + l : first + l + 1, :] for l in locs]
        qs = [normalize(loads[0, :, sp], x) for sp, x in zip(spans, qg)]
        ks = [normalize(loads[1, :, sp], x) for sp, x in zip(spans, kg)]
        vb = [loads[2, :, sp] for sp in spans]
        gb = [loads[3, :, sp] for sp in spans]
        s = [jnp.where(causal, dot_nt(x[2], y[2]), NEG) for x, y in zip(qs, ks)]
        dp = [dot_nt(x, y) for x, y in zip(gb, vb)]
        top = [jnp.max(x, axis=1, keepdims=True) for x in s]
        p = [jnp.exp2((x - t) * LOG_SCALE) for x, t in zip(s, top)]
        total = [jnp.sum(x, axis=1, keepdims=True) for x in p]
        keep = []
        for l in locs:
            kind = (first + l) % 4
            owned = (tile_of_row == (kind & 1)) & (core == (kind >> 1))
            keep.append(jnp.where(owned, 0.0, 1.0))
        p = [x * (z / t) for x, z, t in zip(p, keep, total)]
        w = [x.astype(BF) for x in p]
        rd = [jnp.sum(x.astype(F32) * y, axis=1, keepdims=True) for x, y in zip(w, dp)]
        ds = [(x * (y - z)).astype(BF) for x, y, z in zip(p, dp, rd)]
        dq = [dot_nn(x, y[2]) * SCALE for x, y in zip(ds, ks)]
        dk = [dot_tn(x, y[2]) * SCALE for x, y in zip(ds, qs)]
        dv = [dot_tn(x, y) for x, y in zip(w, gb)]
        for i, (l, sp) in enumerate(zip(locs, spans)):
            stores[0, :, sp] = norm_grad(dq[i], qs[i][0], qs[i][1], qg[i])
            stores[1, :, sp] = norm_grad(dk[i], ks[i][0], ks[i][1], kg[i])
            stores[2, :, sp] = dv[i].astype(BF)
            dk_all[l] = dk[i]
            dv_all[l] = dv[i]
            gains[l : l + 1, :] = jnp.sum(dq[i] * qs[i][0], axis=0, keepdims=True)
            gains[count + l : count + l + 1, :] = jnp.sum(dk[i] * ks[i][0], axis=0, keepdims=True)
        for i, dst in enumerate(outs):
            copy = pltpu.make_async_copy(stores.at[i, :, here], dst.at[:, cols], out_sems.at[n, i])
            copy.start()
            copies.append(copy)
    for j in range(4):
        h0 = 2 * core + 8 * (j >> 1) + 4 * (j & 1)
        h1 = 2 * core + 1 + 8 * (j >> 1) + 4 * (1 - (j & 1))
        for i, (h, e) in enumerate(((h0, 0), (h1, 1), (h1, 0))):
            rows = slice(e * TILE, (e + 1) * TILE)
            part_k[3 * j + i] = dk_all[h, rows, :]
            part_v[3 * j + i] = dv_all[h, rows, :]
    for copy in copies:
        copy.wait()


def owner_kernel(
    c_ref, f0, f3, f2, f1, r0, r2, r3, b3, b2, b1, q_gain, k_gain, home_gains,
    x0, x1, x2, x3, t1, t2, t3, far_k, far_v, gains_out, gains,
):
    c = c_ref[0]
    core, zl, zh, xh = place(c)
    heads = owned_heads(c, 0)
    early = (f0, f1, f2, f3)
    late = (r0, f1.at[pl.ds(2 * TILE, 8 * TILE), :], r2, r3)
    crossed = (b1, b2, b3)
    returned = (x0, x1, x2, x3)
    terms = (t1, t2, t3)
    live = (xh == 1, zh == 1, xh == 1)
    gains[...] = home_gains[...]
    row = lax.broadcasted_iota(jnp.int32, (TILE, 4 * TILE), 0)
    col = lax.broadcasted_iota(jnp.int32, (TILE, 4 * TILE), 1)
    block = col >> 6
    lower = (col & (TILE - 1)) <= row
    far_block = lax.broadcasted_iota(jnp.int32, (1, 6 * TILE), 1) >> 7
    bias = [jnp.where(x, 0.0, NEG) for x in live]
    far_bias = jnp.where(far_block == 0, bias[0], jnp.where(far_block == 1, bias[1], bias[2]))

    def rows_of(ref, tile):
        return ref[tile * TILE : (tile + 1) * TILE, :]

    both = (0, 1)
    order = ((0, 2, 1, 3), (1, 3, 0, 2))
    qg = [q_gain[pl.ds(h, 1), :] for h in heads]
    kg = [k_gain[pl.ds(h, 1), :] for h in heads]


    def stack(e, t):
        parts = []
        for a, i in enumerate(order[e]):
            if a < 2:
                parts.append(rows_of(late[i], t) if t < 2 else rows_of(early[i], t - 2))
            else:
                parts.append(rows_of(late[i], 2 + t))
        return jnp.concatenate(parts, axis=0)

    qs = [normalize(stack(e, 0), qg[e]) for e in both]
    gb = [stack(e, 1) for e in both]
    ks = [normalize(stack(e, 2), kg[e]) for e in both]
    vb = [stack(e, 3) for e in both]
    cross = lambda e, t: jnp.concatenate(
        [rows_of(b, 4 * e + t + 2 * i) for b in crossed for i in range(2)], axis=0
    )
    kf = [normalize(cross(e, 0), kg[e]) for e in both]
    vf = [cross(e, 1) for e in both]
    kx = normalize(jnp.concatenate([rows_of(late[i], 6) for i in order[1]], axis=0), kg[1])
    vx = jnp.concatenate([rows_of(late[i], 7) for i in order[1]], axis=0)
    far = slice(0, 2 * TILE)
    tiles = [slice(i * TILE, (i + 1) * TILE) for i in range(4)]

    s_own = [dot_nt(qs[e][2], ks[e][2]) for e in both]
    s_far = [dot_nt(qs[e][2][far], kf[e][2]) + far_bias for e in both]
    s_x = jnp.concatenate([dot_nt(qs[1][2][t], kx[2][t]) for t in tiles], axis=0)
    d_own = [dot_nt(gb[e], vb[e]) for e in both]
    d_far = [dot_nt(gb[e][far], vf[e]) for e in both]
    d_x = jnp.concatenate([dot_nt(gb[1][t], vx[t]) for t in tiles], axis=0)
    count = []
    for e in both:
        rows = []
        for a in range(4):
            value = jnp.zeros((TILE, 4 * TILE), F32)
            for b in range(4):
                if a == b:
                    here = jnp.where(lower, 3.0 if a < 2 else 2.0, 0.0)
                else:
                    earlier = (zl ^ order[e][b]) < (zl ^ order[e][a])
                    here = jnp.where(earlier, 2.0 if a < 2 and b < 2 else 1.0, 0.0)
                value = jnp.where(block == b, here, value)
            rows.append(value)
        count.append(jnp.concatenate(rows, axis=0))
    s_own = [jnp.where(count[e] > 0.0, s_own[e], NEG) for e in both]
    peak = lambda x: jnp.max(x, axis=1, keepdims=True)
    add = lambda x: jnp.sum(x, axis=1, keepdims=True)
    top = [peak(x) for x in s_own]
    top[1] = jnp.maximum(top[1], peak(s_x))
    top_far = [jnp.maximum(top[e][far], peak(s_far[e])) for e in both]
    top = [jnp.concatenate([top_far[e], top[e][2 * TILE :]], axis=0) for e in both]
    p_own = [count[e] * jnp.exp2((s_own[e] - top[e]) * LOG_SCALE) for e in both]
    p_far = [jnp.exp2((s_far[e] - top_far[e]) * LOG_SCALE) for e in both]
    p_x = jnp.exp2((s_x - top[1]) * LOG_SCALE)
    total = [add(x) for x in p_own]
    total[1] = total[1] + add(p_x)
    total_far = [add(x) for x in p_far]
    total = [
        jnp.concatenate([total[e][far] + total_far[e], total[e][2 * TILE :]], axis=0) for e in both
    ]
    scale = [1.0 / x for x in total]
    p_own = [p_own[e] * scale[e] for e in both]
    p_far = [p_far[e] * scale[e][far] for e in both]
    p_x = p_x * scale[1]
    w_own = [x.astype(BF) for x in p_own]
    w_far = [x.astype(BF) for x in p_far]
    w_x = p_x.astype(BF)
    rd = [add(w_own[e].astype(F32) * d_own[e]) for e in both]
    rd[1] = rd[1] + add(w_x.astype(F32) * d_x)
    rd_far = [add(w_far[e].astype(F32) * d_far[e]) for e in both]
    rd = [jnp.concatenate([rd[e][far] + rd_far[e], rd[e][2 * TILE :]], axis=0) for e in both]
    ds_far = [(p_far[e] * (d_far[e] - rd[e][far])).astype(BF) for e in both]
    ds_own = [(p_own[e] * (d_own[e] - rd[e])).astype(BF) for e in both]
    ds_x = (p_x * (d_x - rd[1])).astype(BF)

    dk_far = [dot_tn(ds_far[e], qs[e][2][far]) * SCALE for e in both]
    dv_far = [dot_tn(w_far[e], gb[e][far]) for e in both]
    for e in both:
        for m in range(3):
            rows = slice(m * 128, (m + 1) * 128)
            terms[m][256 * e : 256 * e + 128, :] = dk_far[e][rows].astype(BF)
            terms[m][256 * e + 128 : 256 * e + 256, :] = dv_far[e][rows].astype(BF)
    dq = [dot_nn(ds_own[e], ks[e][2]) for e in both]
    dq_far = [dot_nn(ds_far[e], kf[e][2]) for e in both]
    dq_x = jnp.concatenate([dot_nn(ds_x[t], kx[2][t]) for t in tiles], axis=0)
    dq[1] = dq[1] + dq_x
    dq = [
        jnp.concatenate([dq[e][far] + dq_far[e], dq[e][2 * TILE :]], axis=0) * SCALE for e in both
    ]
    dk = [dot_tn(ds_own[e], qs[e][2]) * SCALE for e in both]
    dv = [dot_tn(w_own[e], gb[e]) for e in both]
    dk_x = [dot_tn(ds_x[t], qs[1][2][t]) * SCALE for t in tiles]
    dv_x = [dot_tn(w_x[t], gb[1][t]) for t in tiles]
    gq = [norm_grad(dq[e], qs[e][0], qs[e][1], qg[e]) for e in both]
    down = lambda x: jnp.sum(x, axis=0, keepdims=True)
    for e in both:
        for a, i in enumerate(order[e]):
            out = returned[i]
            if a < 2:
                out[0:TILE, :] = gq[e][tiles[a]]
                far_k[i] = dk[e][tiles[a]]
                far_v[i] = dv[e][tiles[a]]
            else:
                out[TILE : 2 * TILE, :] = gq[e][tiles[a]]
                out[2 * TILE : 3 * TILE, :] = dk[e][tiles[a]].astype(BF)
                out[3 * TILE : 4 * TILE, :] = dv[e][tiles[a]].astype(BF)
            if e == 1:
                out[4 * TILE : 5 * TILE, :] = dk_x[a].astype(BF)
                out[5 * TILE : 6 * TILE, :] = dv_x[a].astype(BF)
        key_sum = down(dk[e] * ks[e][0]) + down(dk_far[e] * kf[e][0])
        if e == 1:
            key_sum += sum(down(dk_x[a] * kx[0][tiles[a]]) for a in range(4))
        gains[pl.ds(heads[e], 1), :] += down(dq[e] * qs[e][0])
        gains[pl.ds(HEADS + heads[e], 1), :] += key_sum
    high, low = split_gains(gains[...])
    for out in (*terms, gains_out):
        at = out.shape[0] - 64
        out[at : at + 32, :] = high
        out[at + 32 :, :] = low


def return_pack_kernel(far_k, far_v, own, u1, u2, u3, x1, *refs):
    y0, y1, y2, y3 = refs[-4:]
    total = (joined_gains(own) + joined_gains(u2)) + (joined_gains(u1) + joined_gains(u3))
    high, low = split_gains(total)
    for i, y in enumerate((y0, y1, y2, y3)):
        at = 256 * (i & 1) + 64 * (i >> 1)
        dk = far_k[i]
        dv = far_v[i]
        for u in (u1, u2, u3):
            dk += u[at : at + TILE, :].astype(F32)
            dv += u[at + 128 : at + 128 + TILE, :].astype(F32)
        y[0:TILE, :] = dk.astype(BF)
        y[TILE : 2 * TILE, :] = dv.astype(BF)
        at = y.shape[0] - 64
        y[at : at + 32, :] = high
        y[at + 32 :, :] = low
    y1[2 * TILE : 8 * TILE, :] = x1[...]


def gains_kernel(y0, y2, y3, y1, out):
    out[...] = (joined_gains(y0) + joined_gains(y1)) + (joined_gains(y2) + joined_gains(y3))


def after_kernel(x, *refs):
    refs[-1][...] = x[...]


def pair_sum_kernel(mine, other, ready, out):
    out[...] = mine[...] + other[...]


def last_sum_kernel(mine, other, q_out, k_out):
    q_out[...] = mine[0:HEADS, :] + other[0:HEADS, :]
    k_out[...] = mine[HEADS:, :] + other[HEADS:, :]


def final_kernel(
    c_ref, z0, z2, z3, z1, y0, y2, y3, f0, f1, f2, f3, m0, m2, m3,
    part_k, part_v, k_gain, gq_in, gk_in, gv_in,
    gq_out, gk_out, gv_out, ready, done_k, done_v, sems,
):
    c = c_ref[0]
    core, zl, zh, xh = place(c)
    rank = zl ^ (2 * zh)
    copies = []

    def send(src, dst, e, h, n):
        copy = pltpu.make_async_copy(
            src, dst.at[pl.ds(e * TILE, TILE), pl.ds(pl.multiple_of(h * HD, HD), HD)], sems.at[n]
        )
        copy.start()
        copies.append(copy)

    def tile_of(ref, t):
        return ref[t * TILE : (t + 1) * TILE, :]

    y1 = z1.at[pl.ds(2 * TILE, 6 * TILE), :]
    m1 = f1.at[pl.ds(2 * TILE, 8 * TILE), :]
    jobs = []
    for step in range(4):
        heads = owned_heads(c, step)
        far = step & 1
        near = 1 - far
        y = (y0, y1, y2, y3)[step]
        z = (z0, z1, z2, z3)[step]
        f = (f0, f1, f2, f3)[step]
        m = (m0, m1, m2, m3)[step]
        send(y.at[pl.ds(0, TILE), :], gq_out, far, heads[far], 8 * step)
        send(y.at[pl.ds(TILE, TILE), :], gq_out, near, heads[near], 8 * step + 1)
        owner = rank ^ step
        for i, (h, e, back, at, raw) in enumerate((
            (heads[far], far, z, 0, tile_of(f, 0)),
            (heads[near], near, y, 2, tile_of(m, 4)),
            (heads[1], 0, y, 4, tile_of(m, 6)),
        )):
            part = 3 * owner + (far, near, 2)[i]
            jobs.append((3 * step + i, 8 * step + 2 + 2 * i, part, h, e, back, at, raw))
    for n, sem, part, h, e, back, at, raw in jobs:
        done_v[n] = (part_v[part] + tile_of(back, at + 1).astype(F32)).astype(BF)
        send(done_v.at[n], gv_out, e, h, sem + 1)
    kg = [k_gain[pl.ds(job[3], 1), :] for job in jobs]
    ks = [normalize(job[7], x) for job, x in zip(jobs, kg)]
    dk = [
        part_k[part] + tile_of(back, at).astype(F32)
        for n, sem, part, h, e, back, at, raw in jobs
    ]
    done = [norm_grad(x, y[0], y[1], z) for x, y, z in zip(dk, ks, kg)]
    for (n, sem, part, h, e, back, at, raw), x in zip(jobs, done):
        done_k[n] = x
        send(done_k.at[n], gk_out, e, h, sem)
    ready[...] = jnp.zeros_like(ready)
    for copy in copies:
        copy.wait()


def per_device(q_raw, k_raw, values, d_out, q_gain, k_gain):
    ctx_count = lax.axis_size("ctx")
    dp_count = lax.axis_size("dp")
    here = lax.axis_index("ctx").astype(jnp.int32).reshape(1)
    flat = lambda a: a.reshape(ROWS, HEADS * HD)
    q, k, v, g = (
        pltpu.with_memory_space_constraint(flat(a), pltpu.HBM) for a in (q_raw, k_raw, values, d_out)
    )
    qg = q_gain.reshape(HEADS, HD)
    kg = k_gain.reshape(HEADS, HD)
    params = pltpu.CompilerParams(vmem_limit_bytes=48 * 1024 * 1024)
    shape = jax.ShapeDtypeStruct

    def swap(block, axis, mask):
        count = ctx_count if axis == "ctx" else dp_count
        return lax.ppermute(block, axis, [(i, i ^ mask) for i in range(count)])

    steps = (16, 12, 28)

    def by_distance(blocks):
        return [blocks[i] for i in (0, 2, 3, 1)]

    def around(blocks):
        moved = {i: swap(blocks[i], "ctx", 2 * i) for i in (2, 3, 1)}
        return [blocks[0], moved[1], moved[2], moved[3]]

    def pack_call(name, plan, *after):
        return pl.pallas_call(
            functools.partial(pack_kernel, plan),
            in_specs=[smem_spec()] + [hbm_spec()] * 4 + [any_spec()] * len(after),
            out_specs=[any_spec()] * len(plan),
            out_shape=[shape((len(tiles) * TILE, HD), BF) for _, tiles in plan],
            scratch_shapes=[pltpu.SemaphoreType.DMA((sum(len(tiles) for _, tiles in plan),))],
            compiler_params=params,
            name=name,
        )(here, q, k, v, g, *after)

    packed_early = pack_call("pack_early", tuple((i, early_tiles(i)) for i in range(4)))
    early = around(packed_early)
    packed_late = pack_call("pack_late", tuple((i, late_tiles(i)) for i in (0, 2, 3)), early[1])
    late = [packed_late[0], swap(packed_late[1], "ctx", 4), swap(packed_late[2], "ctx", 6)]

    gq_home, gk_home, gv_home, part_k, part_v, home_gains = pl.pallas_call(
        home_kernel,
        in_specs=[smem_spec()] + [hbm_spec()] * 4 + [vmem_spec()] * 2,
        out_specs=[hbm_spec()] * 3 + [vmem_spec()] * 3,
        out_shape=[shape((ROWS, HEADS * HD), BF)] * 3
        + [shape((12, TILE, HD), F32)] * 2
        + [shape((2 * HEADS, HD), F32)],
        scratch_shapes=[
            pltpu.VMEM((4, ROWS, HEADS * HD), BF),
            pltpu.VMEM((3, ROWS, HEADS * HD), BF),
            pltpu.VMEM((HEADS, ROWS, HD), F32),
            pltpu.VMEM((HEADS, ROWS, HD), F32),
            pltpu.SemaphoreType.DMA((2, 4)),
            pltpu.SemaphoreType.DMA((2, 3)),
        ],
        compiler_params=params,
        name="home_slab",
    )(here, q, k, v, g, qg, kg)

    onward = pl.pallas_call(
        forward_pack_kernel,
        in_specs=[any_spec()] * 5,
        out_specs=any_spec(),
        out_shape=shape((8 * TILE, HD), BF),
        scratch_shapes=[pltpu.SemaphoreType.DMA((4,))],
        compiler_params=params,
        name="pack_far_rows",
    )(early[0], early[3], early[2], early[1], packed_late[0])
    moved = {mask: swap(onward, "ctx", mask) for mask in (16, 12, 28)}
    crossed = [moved[mask] for mask in steps]

    outs = pl.pallas_call(
        owner_kernel,
        in_specs=[smem_spec()] + [vmem_spec()] * 13,
        out_specs=[vmem_spec()] * 10,
        out_shape=[shape((6 * TILE, HD), BF)] * 4
        + [shape((9 * TILE, HD), BF)] * 3
        + [shape((4, TILE, HD), F32)] * 2
        + [shape((TILE, HD), BF)],
        scratch_shapes=[pltpu.VMEM((2 * HEADS, HD), F32)],
        compiler_params=params,
        name="owned_heads",
    )(here, early[0], early[3], early[2], early[1], *late, crossed[2], crossed[1], crossed[0], qg, kg, home_gains)
    back_early, terms, far_k, far_v, own_gains = outs[:4], outs[4:7], outs[7], outs[8], outs[9]
    moved = {mask: swap(terms[steps.index(mask)], "ctx", mask) for mask in (28, 12, 16)}
    terms_in = [moved[mask] for mask in steps]

    def pair_sum(x, axis, mask):
        return x + swap(x, axis, mask)

    def quad_sum(x, axis, mask):
        one, two, three = (swap(x, axis, i * mask) for i in (1, 2, 3))
        return (x + one) + (three + two)

    home_early = [back_early[0], swap(back_early[2], "ctx", 4), swap(back_early[3], "ctx", 6)]
    waits = ()
    back_late = pl.pallas_call(
        return_pack_kernel,
        in_specs=[vmem_spec()] * 7 + [any_spec()] * len(waits),
        out_specs=[vmem_spec()] * 4,
        out_shape=[shape((count * TILE, HD), BF) for count in (3, 9, 3, 3)],
        compiler_params=params,
        name="add_far_terms",
    )(far_k, far_v, own_gains, *terms_in[::-1], back_early[1], *waits)
    back_late = list(back_late)
    back_late[2] = pl.pallas_call(
        after_kernel,
        in_specs=[vmem_spec()] + [any_spec()] * 2,
        out_specs=vmem_spec(),
        out_shape=shape(back_late[2].shape, BF),
        compiler_params=params,
        name="after_early",
    )(back_late[2], home_early[1], home_early[2])
    home_late = around(back_late)

    gains = pl.pallas_call(
        gains_kernel,
        in_specs=[vmem_spec()] * 4,
        out_specs=vmem_spec(),
        out_shape=shape((2 * HEADS, HD), F32),
        compiler_params=params,
        name="sum_gains",
    )(*by_distance(home_late))
    gains = quad_sum(gains, "dp", 1)
    other_gains = swap(gains, "dp", 4)
    gq, gk, gv, ready = pl.pallas_call(
        final_kernel,
        in_specs=[smem_spec()] + [vmem_spec()] * 17 + [any_spec()] * 3,
        out_specs=[any_spec()] * 3 + [vmem_spec()],
        out_shape=[shape((ROWS, HEADS * HD), BF)] * 3 + [shape((8, HD), F32)],
        scratch_shapes=[pltpu.VMEM((12, TILE, HD), BF)] * 2 + [pltpu.SemaphoreType.DMA((32,))],
        input_output_aliases={18: 0, 19: 1, 20: 2},
        compiler_params=params,
        name="finish_rows",
    )(
        here, *by_distance(home_late), *home_early, *packed_early, *packed_late,
        part_k, part_v, kg, gq_home, gk_home, gv_home,
    )
    gains = pl.pallas_call(
        pair_sum_kernel,
        in_specs=[vmem_spec()] * 3,
        out_specs=vmem_spec(),
        out_shape=shape((2 * HEADS, HD), F32),
        compiler_params=params,
        name="pair_sum",
    )(gains, other_gains, ready)
    q_sum, k_sum = pl.pallas_call(
        last_sum_kernel,
        in_specs=[vmem_spec()] * 2,
        out_specs=[vmem_spec()] * 2,
        out_shape=[shape((HEADS, HD), F32)] * 2,
        compiler_params=params,
        name="last_sum",
    )(gains, swap(gains, "ctx", 1))

    whole = lambda a: a.reshape(1, ROWS, HEADS * HD)
    return (
        whole(gq),
        whole(gk),
        whole(gv),
        q_sum.reshape(HEADS * HD),
        k_sum.reshape(HEADS * HD),
    )


def solution(mesh):
    rows = P("dp", "ctx", None)
    return jax.shard_map(
        per_device,
        mesh=mesh,
        in_specs=(rows, rows, rows, rows, P(), P()),
        out_specs=(rows, rows, rows, P(), P()),
        check_vma=False,
    )
```

```python
import functools

import jax
import jax.numpy as jnp
from jax import lax
from jax.experimental import pallas as pl
from jax.experimental.pallas import tpu as pltpu
from jax.sharding import PartitionSpec as P

HEADS = 16
HD = 128
TILE = 64
ROWS = 128
EPS = 1e-06
SCALE = HD ** (-0.5)
BF = jnp.bfloat16
F32 = jnp.float32
NEG = -jnp.inf
LOG_SCALE = SCALE * 1.4426950408889634


def vmem_spec():
    return pl.BlockSpec(memory_space=pltpu.VMEM)


def smem_spec():
    return pl.BlockSpec(memory_space=pltpu.SMEM)


def hbm_spec():
    return pl.BlockSpec(memory_space=pltpu.HBM)


def any_spec():
    return pl.BlockSpec(memory_space=pl.ANY)


def place(c):
    core = c & 1
    zl = (c >> 1) & 3
    zh = (c >> 3) & 1
    xh = (c >> 4) & 1
    return core, zl, zh, xh


def owned_heads(c, k):
    core, zl, zh, xh = place(c)
    rank = (zl ^ (2 * zh)) ^ k
    par = rank & 1
    base = 2 * core + 8 * (rank >> 1)
    return base + 4 * par, base + 1 + 4 * (1 - par)


def normalize(raw, gain):
    x = raw.astype(F32)
    inverse = lax.rsqrt(jnp.mean(x * x, axis=-1, keepdims=True) + EPS)
    normed = x * inverse
    return normed, inverse, (normed * gain).astype(BF)


def norm_grad(upstream, normed, inverse, gain):
    weighted = upstream * gain
    inner = jnp.mean(weighted * normed, axis=-1, keepdims=True)
    return (inverse * (weighted - normed * inner)).astype(BF)


def dot_nt(a, b):
    return lax.dot_general(a, b, (((1,), (1,)), ((), ())), preferred_element_type=F32)


def dot_nn(a, b):
    return lax.dot_general(a, b, (((1,), (0,)), ((), ())), preferred_element_type=F32)


def dot_tn(a, b):
    return lax.dot_general(a, b, (((0,), (0,)), ((), ())), preferred_element_type=F32)


def early_tiles(step):
    far = step & 1
    tiles = (("k", far), ("v", far))
    return tiles + late_tiles(step) if step == 1 else tiles


def late_tiles(step):
    far = step & 1
    near = 1 - far
    return (("q", far), ("g", far), ("q", near), ("g", near), ("k", near), ("v", near), ("k", 2), ("v", 2))


def pack_kernel(plan, c_ref, q, k, v, g, *refs):
    outs, sems = refs[-1 - len(plan) : -1], refs[-1]
    sources = {"q": q, "k": k, "v": v, "g": g}
    c = c_ref[0]
    copies = []
    for (step, tiles), out in zip(plan, outs):
        heads = owned_heads(c, step)
        for t, (name, e) in enumerate(tiles):
            row = 0 if e == 2 else e * TILE
            h = heads[min(e, 1)]
            copy = pltpu.make_async_copy(
                sources[name].at[pl.ds(row, TILE), pl.ds(pl.multiple_of(h * HD, HD), HD)],
                out.at[pl.ds(t * TILE, TILE), :],
                sems.at[len(copies)],
            )
            copy.start()
            copies.append(copy)
    for copy in copies:
        copy.wait()


def split_gains(total):
    high = total.astype(BF)
    return high, (total - high.astype(F32)).astype(BF)


def joined_gains(ref):
    at = ref.shape[0] - 64
    return ref[at : at + 32, :].astype(F32) + ref[at + 32 : at + 64, :].astype(F32)


def forward_pack_kernel(f0, f3, f2, f1, ready, out, sems):
    copies = []
    for k, src in enumerate((f0, f2, f1, f3)):
        copy = pltpu.make_async_copy(
            src.at[pl.ds(0, 2 * TILE), :], out.at[pl.ds(2 * k * TILE, 2 * TILE), :], sems.at[k]
        )
        copy.start()
        copies.append(copy)
    for copy in copies:
        copy.wait()


def home_kernel(
    c_ref, q, k, v, g, q_gain, k_gain, gq_out, gk_out, gv_out, part_k, part_v, gains,
    loads, stores, dk_all, dv_all, in_sems, out_sems,
):
    outs = (gq_out, gk_out, gv_out)
    c = c_ref[0]
    core = c & 1
    count = HEADS
    group = 8
    first = 0
    for n in range(count // group):
        cols = pl.ds((first + n * group) * HD, group * HD)
        for i, src in enumerate((q, k, v, g)):
            pltpu.make_async_copy(
                src.at[:, cols], loads.at[i, :, pl.ds(n * group * HD, group * HD)], in_sems.at[n, i]
            ).start()
    row = lax.broadcasted_iota(jnp.int32, (ROWS, ROWS), 0)
    col = lax.broadcasted_iota(jnp.int32, (ROWS, ROWS), 1)
    causal = col <= row
    tile_of_row = lax.broadcasted_iota(jnp.int32, (ROWS, 1), 0) // TILE
    copies = []
    for n in range(count // group):
        cols = pl.ds((first + n * group) * HD, group * HD)
        here = pl.ds(n * group * HD, group * HD)
        for i, src in enumerate((q, k, v, g)):
            pltpu.make_async_copy(src.at[:, cols], loads.at[i, :, here], in_sems.at[n, i]).wait()
        locs = [n * group + i for i in range(group)]
        spans = [slice(l * HD, (l + 1) * HD) for l in locs]
        qg = [q_gain[first + l : first + l + 1, :] for l in locs]
        kg = [k_gain[first + l : first + l + 1, :] for l in locs]
        qs = [normalize(loads[0, :, sp], x) for sp, x in zip(spans, qg)]
        ks = [normalize(loads[1, :, sp], x) for sp, x in zip(spans, kg)]
        vb = [loads[2, :, sp] for sp in spans]
        gb = [loads[3, :, sp] for sp in spans]
        s = [jnp.where(causal, dot_nt(x[2], y[2]), NEG) for x, y in zip(qs, ks)]
        dp = [dot_nt(x, y) for x, y in zip(gb, vb)]
        top = [jnp.max(x, axis=1, keepdims=True) for x in s]
        p = [jnp.exp2((x - t) * LOG_SCALE) for x, t in zip(s, top)]
        total = [jnp.sum(x, axis=1, keepdims=True) for x in p]
        keep = []
        for l in locs:
            kind = (first + l) % 4
            owned = (tile_of_row == (kind & 1)) & (core == (kind >> 1))
            keep.append(jnp.where(owned, 0.0, 1.0))
        p = [x * (z / t) for x, z, t in zip(p, keep, total)]
        w = [x.astype(BF) for x in p]
        rd = [jnp.sum(x.astype(F32) * y, axis=1, keepdims=True) for x, y in zip(w, dp)]
        ds = [(x * (y - z)).astype(BF) for x, y, z in zip(p, dp, rd)]
        dq = [dot_nn(x, y[2]) * SCALE for x, y in zip(ds, ks)]
        dk = [dot_tn(x, y[2]) * SCALE for x, y in zip(ds, qs)]
        dv = [dot_tn(x, y) for x, y in zip(w, gb)]
        for i, (l, sp) in enumerate(zip(locs, spans)):
            stores[0, :, sp] = norm_grad(dq[i], qs[i][0], qs[i][1], qg[i])
            stores[1, :, sp] = norm_grad(dk[i], ks[i][0], ks[i][1], kg[i])
            stores[2, :, sp] = dv[i].astype(BF)
            dk_all[l] = dk[i]
            dv_all[l] = dv[i]
            gains[l : l + 1, :] = jnp.sum(dq[i] * qs[i][0], axis=0, keepdims=True)
            gains[count + l : count + l + 1, :] = jnp.sum(dk[i] * ks[i][0], axis=0, keepdims=True)
        for i, dst in enumerate(outs):
            copy = pltpu.make_async_copy(stores.at[i, :, here], dst.at[:, cols], out_sems.at[n, i])
            copy.start()
            copies.append(copy)
    for j in range(4):
        h0 = 2 * core + 8 * (j >> 1) + 4 * (j & 1)
        h1 = 2 * core + 1 + 8 * (j >> 1) + 4 * (1 - (j & 1))
        for i, (h, e) in enumerate(((h0, 0), (h1, 1), (h1, 0))):
            rows = slice(e * TILE, (e + 1) * TILE)
            part_k[3 * j + i] = dk_all[h, rows, :]
            part_v[3 * j + i] = dv_all[h, rows, :]
    for copy in copies:
        copy.wait()


def owner_kernel(
    c_ref, f0, f3, f2, f1, r0, r2, r3, b2, b3, b1, q_gain, k_gain, home_gains,
    x0, x1, x2, x3, t1, t2, t3, far_k, far_v, gains_out, gains,
):
    c = c_ref[0]
    core, zl, zh, xh = place(c)
    heads = owned_heads(c, 0)
    early = (f0, f1, f2, f3)
    late = (r0, f1.at[pl.ds(2 * TILE, 8 * TILE), :], r2, r3)
    crossed = (b1, b2, b3)
    returned = (x0, x1, x2, x3)
    terms = (t1, t2, t3)
    live = (xh == 1, zh == 1, xh == 1)
    gains[...] = home_gains[...]
    row = lax.broadcasted_iota(jnp.int32, (TILE, 4 * TILE), 0)
    col = lax.broadcasted_iota(jnp.int32, (TILE, 4 * TILE), 1)
    block = col >> 6
    lower = (col & (TILE - 1)) <= row
    far_block = lax.broadcasted_iota(jnp.int32, (1, 6 * TILE), 1) >> 7
    bias = [jnp.where(x, 0.0, NEG) for x in live]
    far_bias = jnp.where(far_block == 0, bias[0], jnp.where(far_block == 1, bias[1], bias[2]))

    def rows_of(ref, tile):
        return ref[tile * TILE : (tile + 1) * TILE, :]

    both = (0, 1)
    order = ((0, 2, 1, 3), (1, 3, 0, 2))
    qg = [q_gain[pl.ds(h, 1), :] for h in heads]
    kg = [k_gain[pl.ds(h, 1), :] for h in heads]


    def stack(e, t):
        parts = []
        for a, i in enumerate(order[e]):
            if a < 2:
                parts.append(rows_of(late[i], t) if t < 2 else rows_of(early[i], t - 2))
            else:
                parts.append(rows_of(late[i], 2 + t))
        return jnp.concatenate(parts, axis=0)

    qs = [normalize(stack(e, 0), qg[e]) for e in both]
    gb = [stack(e, 1) for e in both]
    ks = [normalize(stack(e, 2), kg[e]) for e in both]
    vb = [stack(e, 3) for e in both]
    cross = lambda e, t: jnp.concatenate(
        [rows_of(b, 4 * e + t + 2 * i) for b in crossed for i in range(2)], axis=0
    )
    kf = [normalize(cross(e, 0), kg[e]) for e in both]
    vf = [cross(e, 1) for e in both]
    kx = normalize(jnp.concatenate([rows_of(late[i], 6) for i in order[1]], axis=0), kg[1])
    vx = jnp.concatenate([rows_of(late[i], 7) for i in order[1]], axis=0)
    far = slice(0, 2 * TILE)
    tiles = [slice(i * TILE, (i + 1) * TILE) for i in range(4)]

    s_own = [dot_nt(qs[e][2], ks[e][2]) for e in both]
    s_far = [dot_nt(qs[e][2][far], kf[e][2]) + far_bias for e in both]
    s_x = jnp.concatenate([dot_nt(qs[1][2][t], kx[2][t]) for t in tiles], axis=0)
    d_own = [dot_nt(gb[e], vb[e]) for e in both]
    d_far = [dot_nt(gb[e][far], vf[e]) for e in both]
    d_x = jnp.concatenate([dot_nt(gb[1][t], vx[t]) for t in tiles], axis=0)
    count = []
    for e in both:
        rows = []
        for a in range(4):
            value = jnp.zeros((TILE, 4 * TILE), F32)
            for b in range(4):
                if a == b:
                    here = jnp.where(lower, 3.0 if a < 2 else 2.0, 0.0)
                else:
                    earlier = (zl ^ order[e][b]) < (zl ^ order[e][a])
                    here = jnp.where(earlier, 2.0 if a < 2 and b < 2 else 1.0, 0.0)
                value = jnp.where(block == b, here, value)
            rows.append(value)
        count.append(jnp.concatenate(rows, axis=0))
    s_own = [jnp.where(count[e] > 0.0, s_own[e], NEG) for e in both]
    peak = lambda x: jnp.max(x, axis=1, keepdims=True)
    add = lambda x: jnp.sum(x, axis=1, keepdims=True)
    top = [peak(x) for x in s_own]
    top[1] = jnp.maximum(top[1], peak(s_x))
    top_far = [jnp.maximum(top[e][far], peak(s_far[e])) for e in both]
    top = [jnp.concatenate([top_far[e], top[e][2 * TILE :]], axis=0) for e in both]
    p_own = [count[e] * jnp.exp2((s_own[e] - top[e]) * LOG_SCALE) for e in both]
    p_far = [jnp.exp2((s_far[e] - top_far[e]) * LOG_SCALE) for e in both]
    p_x = jnp.exp2((s_x - top[1]) * LOG_SCALE)
    total = [add(x) for x in p_own]
    total[1] = total[1] + add(p_x)
    total_far = [add(x) for x in p_far]
    total = [
        jnp.concatenate([total[e][far] + total_far[e], total[e][2 * TILE :]], axis=0) for e in both
    ]
    scale = [1.0 / x for x in total]
    p_own = [p_own[e] * scale[e] for e in both]
    p_far = [p_far[e] * scale[e][far] for e in both]
    p_x = p_x * scale[1]
    w_own = [x.astype(BF) for x in p_own]
    w_far = [x.astype(BF) for x in p_far]
    w_x = p_x.astype(BF)
    rd = [add(w_own[e].astype(F32) * d_own[e]) for e in both]
    rd[1] = rd[1] + add(w_x.astype(F32) * d_x)
    rd_far = [add(w_far[e].astype(F32) * d_far[e]) for e in both]
    rd = [jnp.concatenate([rd[e][far] + rd_far[e], rd[e][2 * TILE :]], axis=0) for e in both]
    ds_far = [(p_far[e] * (d_far[e] - rd[e][far])).astype(BF) for e in both]
    ds_own = [(p_own[e] * (d_own[e] - rd[e])).astype(BF) for e in both]
    ds_x = (p_x * (d_x - rd[1])).astype(BF)

    dk_far = [dot_tn(ds_far[e], qs[e][2][far]) * SCALE for e in both]
    dv_far = [dot_tn(w_far[e], gb[e][far]) for e in both]
    for e in both:
        for m in range(3):
            rows = slice(m * 128, (m + 1) * 128)
            terms[m][256 * e : 256 * e + 128, :] = dk_far[e][rows].astype(BF)
            terms[m][256 * e + 128 : 256 * e + 256, :] = dv_far[e][rows].astype(BF)
    dq = [dot_nn(ds_own[e], ks[e][2]) for e in both]
    dq_far = [dot_nn(ds_far[e], kf[e][2]) for e in both]
    dq_x = jnp.concatenate([dot_nn(ds_x[t], kx[2][t]) for t in tiles], axis=0)
    dq[1] = dq[1] + dq_x
    dq = [
        jnp.concatenate([dq[e][far] + dq_far[e], dq[e][2 * TILE :]], axis=0) * SCALE for e in both
    ]
    dk = [dot_tn(ds_own[e], qs[e][2]) * SCALE for e in both]
    dv = [dot_tn(w_own[e], gb[e]) for e in both]
    dk_x = [dot_tn(ds_x[t], qs[1][2][t]) * SCALE for t in tiles]
    dv_x = [dot_tn(w_x[t], gb[1][t]) for t in tiles]
    gq = [norm_grad(dq[e], qs[e][0], qs[e][1], qg[e]) for e in both]
    down = lambda x: jnp.sum(x, axis=0, keepdims=True)
    for e in both:
        for a, i in enumerate(order[e]):
            out = returned[i]
            if a < 2:
                out[0:TILE, :] = gq[e][tiles[a]]
                far_k[i] = dk[e][tiles[a]]
                far_v[i] = dv[e][tiles[a]]
            else:
                out[TILE : 2 * TILE, :] = gq[e][tiles[a]]
                out[2 * TILE : 3 * TILE, :] = dk[e][tiles[a]].astype(BF)
                out[3 * TILE : 4 * TILE, :] = dv[e][tiles[a]].astype(BF)
            if e == 1:
                out[4 * TILE : 5 * TILE, :] = dk_x[a].astype(BF)
                out[5 * TILE : 6 * TILE, :] = dv_x[a].astype(BF)
        key_sum = down(dk[e] * ks[e][0]) + down(dk_far[e] * kf[e][0])
        if e == 1:
            key_sum += sum(down(dk_x[a] * kx[0][tiles[a]]) for a in range(4))
        gains[pl.ds(heads[e], 1), :] += down(dq[e] * qs[e][0])
        gains[pl.ds(HEADS + heads[e], 1), :] += key_sum
    high, low = split_gains(gains[...])
    for out in (*terms, gains_out):
        at = out.shape[0] - 64
        out[at : at + 32, :] = high
        out[at + 32 :, :] = low


def return_pack_kernel(far_k, far_v, own, u1, u2, u3, x1, *refs):
    y0, y1, y2, y3 = refs[-4:]
    total = (joined_gains(own) + joined_gains(u2)) + (joined_gains(u1) + joined_gains(u3))
    high, low = split_gains(total)
    for i, y in enumerate((y0, y1, y2, y3)):
        at = 256 * (i & 1) + 64 * (i >> 1)
        dk = far_k[i]
        dv = far_v[i]
        for u in (u1, u2, u3):
            dk += u[at : at + TILE, :].astype(F32)
            dv += u[at + 128 : at + 128 + TILE, :].astype(F32)
        y[0:TILE, :] = dk.astype(BF)
        y[TILE : 2 * TILE, :] = dv.astype(BF)
        at = y.shape[0] - 64
        y[at : at + 32, :] = high
        y[at + 32 :, :] = low
    y1[2 * TILE : 8 * TILE, :] = x1[...]


def gains_kernel(y0, y2, y3, y1, out):
    out[...] = (joined_gains(y0) + joined_gains(y1)) + (joined_gains(y2) + joined_gains(y3))


def after_kernel(x, *refs):
    refs[-1][...] = x[...]


def pair_sum_kernel(mine, other, ready, out):
    out[...] = mine[...] + other[...]


def last_sum_kernel(mine, other, q_out, k_out):
    q_out[...] = mine[0:HEADS, :] + other[0:HEADS, :]
    k_out[...] = mine[HEADS:, :] + other[HEADS:, :]


def final_kernel(
    c_ref, z0, z2, z3, z1, y0, y2, y3, f0, f1, f2, f3, m0, m2, m3,
    part_k, part_v, k_gain, gq_in, gk_in, gv_in,
    gq_out, gk_out, gv_out, ready, done_k, done_v, sems,
):
    c = c_ref[0]
    core, zl, zh, xh = place(c)
    rank = zl ^ (2 * zh)
    copies = []

    def send(src, dst, e, h, n):
        copy = pltpu.make_async_copy(
            src, dst.at[pl.ds(e * TILE, TILE), pl.ds(pl.multiple_of(h * HD, HD), HD)], sems.at[n]
        )
        copy.start()
        copies.append(copy)

    def tile_of(ref, t):
        return ref[t * TILE : (t + 1) * TILE, :]

    y1 = z1.at[pl.ds(2 * TILE, 6 * TILE), :]
    m1 = f1.at[pl.ds(2 * TILE, 8 * TILE), :]
    jobs = []
    for step in range(4):
        heads = owned_heads(c, step)
        far = step & 1
        near = 1 - far
        y = (y0, y1, y2, y3)[step]
        z = (z0, z1, z2, z3)[step]
        f = (f0, f1, f2, f3)[step]
        m = (m0, m1, m2, m3)[step]
        send(y.at[pl.ds(0, TILE), :], gq_out, far, heads[far], 8 * step)
        send(y.at[pl.ds(TILE, TILE), :], gq_out, near, heads[near], 8 * step + 1)
        owner = rank ^ step
        for i, (h, e, back, at, raw) in enumerate((
            (heads[far], far, z, 0, tile_of(f, 0)),
            (heads[near], near, y, 2, tile_of(m, 4)),
            (heads[1], 0, y, 4, tile_of(m, 6)),
        )):
            part = 3 * owner + (far, near, 2)[i]
            jobs.append((3 * step + i, 8 * step + 2 + 2 * i, part, h, e, back, at, raw))
    for n, sem, part, h, e, back, at, raw in jobs:
        done_v[n] = (part_v[part] + tile_of(back, at + 1).astype(F32)).astype(BF)
        send(done_v.at[n], gv_out, e, h, sem + 1)
    kg = [k_gain[pl.ds(job[3], 1), :] for job in jobs]
    ks = [normalize(job[7], x) for job, x in zip(jobs, kg)]
    dk = [
        part_k[part] + tile_of(back, at).astype(F32)
        for n, sem, part, h, e, back, at, raw in jobs
    ]
    done = [norm_grad(x, y[0], y[1], z) for x, y, z in zip(dk, ks, kg)]
    for (n, sem, part, h, e, back, at, raw), x in zip(jobs, done):
        done_k[n] = x
        send(done_k.at[n], gk_out, e, h, sem)
    ready[...] = jnp.zeros_like(ready)
    for copy in copies:
        copy.wait()


def per_device(q_raw, k_raw, values, d_out, q_gain, k_gain):
    ctx_count = lax.axis_size("ctx")
    dp_count = lax.axis_size("dp")
    here = lax.axis_index("ctx").astype(jnp.int32).reshape(1)
    flat = lambda a: a.reshape(ROWS, HEADS * HD)
    q, k, v, g = (
        pltpu.with_memory_space_constraint(flat(a), pltpu.HBM) for a in (q_raw, k_raw, values, d_out)
    )
    qg = q_gain.reshape(HEADS, HD)
    kg = k_gain.reshape(HEADS, HD)
    params = pltpu.CompilerParams(vmem_limit_bytes=48 * 1024 * 1024)
    shape = jax.ShapeDtypeStruct

    def swap(block, axis, mask):
        count = ctx_count if axis == "ctx" else dp_count
        return lax.ppermute(block, axis, [(i, i ^ mask) for i in range(count)])

    steps = (16, 12, 28)

    def by_distance(blocks):
        return [blocks[i] for i in (0, 2, 3, 1)]

    def around(blocks):
        moved = {i: swap(blocks[i], "ctx", 2 * i) for i in (2, 3, 1)}
        return [blocks[0], moved[1], moved[2], moved[3]]

    def pack_call(name, plan, *after):
        return pl.pallas_call(
            functools.partial(pack_kernel, plan),
            in_specs=[smem_spec()] + [hbm_spec()] * 4 + [any_spec()] * len(after),
            out_specs=[any_spec()] * len(plan),
            out_shape=[shape((len(tiles) * TILE, HD), BF) for _, tiles in plan],
            scratch_shapes=[pltpu.SemaphoreType.DMA((sum(len(tiles) for _, tiles in plan),))],
            compiler_params=params,
            name=name,
        )(here, q, k, v, g, *after)

    packed_early = pack_call("pack_early", tuple((i, early_tiles(i)) for i in range(4)))
    early = around(packed_early)
    packed_late = pack_call("pack_late", tuple((i, late_tiles(i)) for i in (0, 2, 3)), early[1])
    late = [packed_late[0], swap(packed_late[1], "ctx", 4), swap(packed_late[2], "ctx", 6)]

    gq_home, gk_home, gv_home, part_k, part_v, home_gains = pl.pallas_call(
        home_kernel,
        in_specs=[smem_spec()] + [hbm_spec()] * 4 + [vmem_spec()] * 2,
        out_specs=[hbm_spec()] * 3 + [vmem_spec()] * 3,
        out_shape=[shape((ROWS, HEADS * HD), BF)] * 3
        + [shape((12, TILE, HD), F32)] * 2
        + [shape((2 * HEADS, HD), F32)],
        scratch_shapes=[
            pltpu.VMEM((4, ROWS, HEADS * HD), BF),
            pltpu.VMEM((3, ROWS, HEADS * HD), BF),
            pltpu.VMEM((HEADS, ROWS, HD), F32),
            pltpu.VMEM((HEADS, ROWS, HD), F32),
            pltpu.SemaphoreType.DMA((2, 4)),
            pltpu.SemaphoreType.DMA((2, 3)),
        ],
        compiler_params=params,
        name="home_slab",
    )(here, q, k, v, g, qg, kg)

    onward = pl.pallas_call(
        forward_pack_kernel,
        in_specs=[any_spec()] * 5,
        out_specs=any_spec(),
        out_shape=shape((8 * TILE, HD), BF),
        scratch_shapes=[pltpu.SemaphoreType.DMA((4,))],
        compiler_params=params,
        name="pack_far_rows",
    )(early[0], early[3], early[2], early[1], packed_late[0])
    moved = {mask: swap(onward, "ctx", mask) for mask in (16, 12, 28)}
    crossed = [moved[mask] for mask in steps]

    outs = pl.pallas_call(
        owner_kernel,
        in_specs=[smem_spec()] + [vmem_spec()] * 13,
        out_specs=[vmem_spec()] * 10,
        out_shape=[shape((6 * TILE, HD), BF)] * 4
        + [shape((9 * TILE, HD), BF)] * 3
        + [shape((4, TILE, HD), F32)] * 2
        + [shape((TILE, HD), BF)],
        scratch_shapes=[pltpu.VMEM((2 * HEADS, HD), F32)],
        compiler_params=params,
        name="owned_heads",
    )(here, early[0], early[3], early[2], early[1], *late, crossed[1], crossed[2], crossed[0], qg, kg, home_gains)
    back_early, terms, far_k, far_v, own_gains = outs[:4], outs[4:7], outs[7], outs[8], outs[9]
    moved = {mask: swap(terms[steps.index(mask)], "ctx", mask) for mask in (28, 12, 16)}
    terms_in = [moved[mask] for mask in steps]

    def pair_sum(x, axis, mask):
        return x + swap(x, axis, mask)

    def quad_sum(x, axis, mask):
        one, two, three = (swap(x, axis, i * mask) for i in (1, 2, 3))
        return (x + one) + (three + two)

    home_early = [back_early[0], swap(back_early[2], "ctx", 4), swap(back_early[3], "ctx", 6)]
    waits = ()
    back_late = pl.pallas_call(
        return_pack_kernel,
        in_specs=[vmem_spec()] * 7 + [any_spec()] * len(waits),
        out_specs=[vmem_spec()] * 4,
        out_shape=[shape((count * TILE, HD), BF) for count in (3, 9, 3, 3)],
        compiler_params=params,
        name="add_far_terms",
    )(far_k, far_v, own_gains, *terms_in[::-1], back_early[1], *waits)
    back_late = list(back_late)
    back_late[2] = pl.pallas_call(
        after_kernel,
        in_specs=[vmem_spec()] + [any_spec()] * 2,
        out_specs=vmem_spec(),
        out_shape=shape(back_late[2].shape, BF),
        compiler_params=params,
        name="after_early",
    )(back_late[2], home_early[1], home_early[2])
    home_late = around(back_late)

    gains = pl.pallas_call(
        gains_kernel,
        in_specs=[vmem_spec()] * 4,
        out_specs=vmem_spec(),
        out_shape=shape((2 * HEADS, HD), F32),
        compiler_params=params,
        name="sum_gains",
    )(*by_distance(home_late))
    gains = quad_sum(gains, "dp", 1)
    other_gains = swap(gains, "dp", 4)
    gq, gk, gv, ready = pl.pallas_call(
        final_kernel,
        in_specs=[smem_spec()] + [vmem_spec()] * 17 + [any_spec()] * 3,
        out_specs=[any_spec()] * 3 + [vmem_spec()],
        out_shape=[shape((ROWS, HEADS * HD), BF)] * 3 + [shape((8, HD), F32)],
        scratch_shapes=[pltpu.VMEM((12, TILE, HD), BF)] * 2 + [pltpu.SemaphoreType.DMA((32,))],
        input_output_aliases={18: 0, 19: 1, 20: 2},
        compiler_params=params,
        name="finish_rows",
    )(
        here, *by_distance(home_late), *home_early, *packed_early, *packed_late,
        part_k, part_v, kg, gq_home, gk_home, gv_home,
    )
    gains = pl.pallas_call(
        pair_sum_kernel,
        in_specs=[vmem_spec()] * 3,
        out_specs=vmem_spec(),
        out_shape=shape((2 * HEADS, HD), F32),
        compiler_params=params,
        name="pair_sum",
    )(gains, other_gains, ready)
    q_sum, k_sum = pl.pallas_call(
        last_sum_kernel,
        in_specs=[vmem_spec()] * 2,
        out_specs=[vmem_spec()] * 2,
        out_shape=[shape((HEADS, HD), F32)] * 2,
        compiler_params=params,
        name="last_sum",
    )(gains, swap(gains, "ctx", 1))

    whole = lambda a: a.reshape(1, ROWS, HEADS * HD)
    return (
        whole(gq),
        whole(gk),
        whole(gv),
        q_sum.reshape(HEADS * HD),
        k_sum.reshape(HEADS * HD),
    )


def solution(mesh):
    rows = P("dp", "ctx", None)
    return jax.shard_map(
        per_device,
        mesh=mesh,
        in_specs=(rows, rows, rows, rows, P(), P()),
        out_specs=(rows, rows, rows, P(), P()),
        check_vma=False,
    )
```
